512 devices in a mesh: ctx: 128 (over x, z, y_hi), mp: 4 (over y_lo, core).
Axes of the slice: x: 4, y: 8 (y_hi: 4, y_lo: 2; y = y_hi * 2 + y_lo), z: 8, core: 2. Of those that a mesh axis runs over, the one named last changes fastest.
Arguments:
- q_in: bfloat16 [17408, 8192], P('ctx', 'mp'), may hold values from -6 to 6
- k_in: bfloat16 [17408, 8192], P('ctx', 'mp'), may hold values from -6 to 6
- value_projected: bfloat16 [17408, 8192], P('ctx', 'mp'), may hold values from -6 to 6
- grad_out: bfloat16 [17408, 8192], P('ctx', 'mp'), may hold values from -6 to 6
- filt_short: bfloat16 [7, 512], P(None, 'ctx'), may hold values from -2 to 2
- filt_medium: bfloat16 [128, 512], P(None, 'ctx'), may hold values from -0.5 to 0.5
Outputs:
- grad_q: bfloat16 [17408, 8192], P('ctx', 'mp')
- grad_k: bfloat16 [17408, 8192], P('ctx', 'mp')
- grad_v: bfloat16 [17408, 8192], P('ctx', 'mp')
- grad_filt_short: float32 [7, 512], P(None, 'ctx')
- grad_filt_medium: float32 [128, 512], P(None, 'ctx')
The draws below stay inside these ranges and needn't reach their ends.
All inputs are finite; a program needn't handle non-finite values.
Results may differ from the reference program's by a relative error of at most 0.02.
Values may be sent and summed in bfloat16 or wider, within the bound.
No kernel may reach another device: no remote copies, remote signals or barrier semaphores. Data moves between devices by JAX's collectives and lax.ppermute only.
A program may use at most 128 MiB of HBM per device.

```python
import jax
import jax.numpy as jnp
from jax import lax

D = 8192
G = 512
FEATURIZER_TAPS = 7
KB = 128
CPG = 16
TOKENS = 17408


def shard_levels(key, shape, cuts, low, high):
    factor_of = 1.0
    for axis_at, blocks in cuts:
        draws = jax.random.uniform(jax.random.fold_in(jax.random.fold_in(key, 6), axis_at), (blocks,), jnp.float32, low / len(cuts), high / len(cuts))
        factor_of = factor_of * jnp.repeat(jnp.exp(draws), shape[axis_at] // blocks).reshape((-1,) + (1,) * (len(shape) - 1 - axis_at))
    return factor_of


def scatter_about(own_key, dims, deviation, bound, cuts=(), held_as=jnp.bfloat16):
    entries = jax.random.normal(own_key, dims, jnp.float32) * deviation
    if len(cuts) > 0:
        entries = shard_levels(own_key, dims, cuts, -0.22, 0.18) * entries
    return jnp.clip(entries, min=-bound, max=bound).astype(held_as)


def setup_inputs(seed: int = 0) -> dict:
    streams_of = jax.random.split(jax.random.key(seed), 7)
    return {
        "q_in": scatter_about(streams_of[0], (TOKENS, D), 1.0, 6.0, ((0, 128), (1, 4))),
        "k_in": scatter_about(streams_of[1], (TOKENS, D), 1.0, 6.0, ((0, 128), (1, 4))),
        "value_projected": scatter_about(streams_of[2], (TOKENS, D), 1.0, 6.0, ((0, 128), (1, 4))),
        "grad_out": scatter_about(streams_of[3], (TOKENS, D), 1.0, 6.0, ((0, 128), (1, 4))),
        "filt_short": scatter_about(streams_of[4], (FEATURIZER_TAPS, G), FEATURIZER_TAPS ** -0.5, 2.0, ((1, 128),)),
        "filt_medium": scatter_about(streams_of[5], (KB, G), KB ** -0.5, 0.5, ((1, 128),)),
    }


def expand_taps(taps):
    return jnp.repeat(taps.astype(jnp.float32), CPG, axis=1)


def causal_filter(signal, taps):
    count = taps.shape[0]
    length = signal.shape[0]
    expanded = expand_taps(taps)
    padded = jnp.concatenate([jnp.zeros((count - 1, signal.shape[1]), jnp.float32), signal.astype(jnp.float32)], 0)

    def add_tap(tap_index, running):
        start = (count - 1 - tap_index).astype(jnp.int32)
        return running + expanded[tap_index] * lax.dynamic_slice_in_dim(padded, start, length, 0)

    return lax.fori_loop(0, count, add_tap, jnp.zeros(signal.shape, jnp.float32))


def anticausal_filter(signal, taps):
    count = taps.shape[0]
    length = signal.shape[0]
    expanded = expand_taps(taps)
    padded = jnp.concatenate([signal.astype(jnp.float32), jnp.zeros((count - 1, signal.shape[1]), jnp.float32)], 0)

    def add_tap(tap_index, running):
        start = tap_index.astype(jnp.int32)
        return running + expanded[tap_index] * lax.dynamic_slice_in_dim(padded, start, length, 0)

    return lax.fori_loop(0, count, add_tap, jnp.zeros(signal.shape, jnp.float32))


def filter_gradient(grad, signal, count):
    length = signal.shape[0]
    padded = jnp.concatenate([jnp.zeros((count - 1, signal.shape[1]), jnp.float32), signal.astype(jnp.float32)], 0)
    grad_wide = grad.astype(jnp.float32)

    def one_tap(tap_index):
        start = (count - 1 - tap_index).astype(jnp.int32)
        shifted = lax.dynamic_slice_in_dim(padded, start, length, 0)
        return jnp.sum(grad_wide * shifted, 0).reshape(-1, CPG).sum(1)

    return lax.map(one_tap, jnp.arange(count).astype(jnp.int32))


def reference(q_in, k_in, value_projected, grad_out, filt_short, filt_medium):
    f32 = jnp.float32
    brain_float_half = jnp.bfloat16
    q_feat = causal_filter(q_in, filt_short).astype(brain_float_half)
    k_feat = causal_filter(k_in, filt_short).astype(brain_float_half)
    value_featurized = causal_filter(value_projected, filt_short).astype(brain_float_half)
    u_inner = (k_feat.astype(f32) * value_featurized.astype(f32)).astype(brain_float_half)
    z_inner = causal_filter(u_inner, filt_medium)
    d_inner = (grad_out.astype(f32) * q_feat.astype(f32)).astype(brain_float_half)
    du_inner = anticausal_filter(d_inner, filt_medium)
    dq_feat = (grad_out.astype(f32) * z_inner).astype(brain_float_half)
    dk_feat = (du_inner * value_featurized.astype(f32)).astype(brain_float_half)
    value_featurized_gradient = (du_inner * k_feat.astype(f32)).astype(brain_float_half)
    grad_q = anticausal_filter(dq_feat, filt_short).astype(brain_float_half)
    grad_k = anticausal_filter(dk_feat, filt_short).astype(brain_float_half)
    grad_v = anticausal_filter(value_featurized_gradient, filt_short).astype(brain_float_half)
    grad_filt_medium = filter_gradient(d_inner, u_inner, KB)
    grad_filt_short = (filter_gradient(dq_feat, q_in, FEATURIZER_TAPS) + filter_gradient(dk_feat, k_in, FEATURIZER_TAPS)
                       + filter_gradient(value_featurized_gradient, value_projected, FEATURIZER_TAPS))
    return (grad_q, grad_k, grad_v, grad_filt_short, grad_filt_medium)
```

```python
import jax
import jax.numpy as jnp
from jax import lax
from jax.experimental import pallas as pl
from jax.experimental.pallas import tpu as pltpu
from jax.sharding import Mesh, PartitionSpec as P

F32 = jnp.float32
BF16 = jnp.bfloat16
CPG = 16
KS = 7
KB = 128
LANES = 128
GPB = LANES // CPG
HALO = 8
CTX = ("x", "z", "yh")
MP = ("yl", "core")
ALL = CTX + MP
SIZES = (4, 8, 4, 4)
VMEM = 56 * 1024 * 1024


def params(**more):
    return pltpu.CompilerParams(vmem_limit_bytes=VMEM, **more)


def lane_group(shape):
    return lax.broadcasted_iota(jnp.int32, shape, len(shape) - 1) // CPG


def short_taps(taps):
    row = lax.broadcasted_iota(jnp.int32, (16, LANES), 0)
    group = jnp.where(row % 8 >= 4, row // 8 * 4 + row % 4, -1)
    spread = (lane_group((16, LANES)) == group).astype(F32)
    return lax.dot_general(
        taps[:, :LANES].T, spread, (((1,), (0,)), ((), ())), precision=lax.Precision.HIGHEST,
        preferred_element_type=F32,
    )[:8]


def load_rows(scratch, first, second):
    cut = first.shape[0]
    scratch[0:cut] = first
    scratch[cut : cut + second.shape[0]] = second


def featurize_kernel(q, k, v, g, before, taps, u, d, kf, vf, u_send, d_send, hexp, pad):
    rows = q.shape[0]
    for b in range(q.shape[1] // LANES):
        lanes = slice(b * LANES, (b + 1) * LANES)
        both = taps[2 * b : 2 * b + 2].astype(F32).reshape(16, LANES)
        h = short_taps(both)
        hexp[:, lanes] = h
        early = before[:, lanes].astype(F32)
        feats = []
        for i, x in enumerate((q, k, v)):
            slot = pad.at[(3 * b + i) % 2]
            load_rows(slot, early[8 * i : 8 * i + 8], x[:, lanes].astype(F32))
            total = h[0:1] * slot[HALO : HALO + rows]
            for j in range(1, KS):
                total = total + h[j : j + 1] * slot[HALO - j : HALO - j + rows]
            feats.append(total.astype(BF16).astype(F32))
        qf, kfeat, vfeat = feats
        kf[:, lanes] = kfeat.astype(BF16)
        vf[:, lanes] = vfeat.astype(BF16)
        inner = kfeat * vfeat
        u[:, lanes] = inner.astype(BF16)
        u_send[:, lanes] = inner[rows - KB :].astype(BF16)
        gated = g[:, lanes].astype(F32) * qf
        d[:, lanes] = gated.astype(BF16)
        d_send[:, lanes] = gated[:KB].astype(BF16)


def featurize(q, k, v, g, before, taps, interpret=False):
    rows, channels = q.shape
    wide = 512
    block = lambda r: pl.BlockSpec((r, wide), lambda i: (0, i))
    shape = lambda r, t=BF16: jax.ShapeDtypeStruct((r, channels), t)
    return pl.pallas_call(
        featurize_kernel,
        grid=(channels // wide,),
        in_specs=[block(rows)] * 4
        + [block(24), pl.BlockSpec((2 * wide // LANES, 8, LANES), lambda i: (i, 0, 0))],
        out_specs=[block(rows)] * 4 + [block(KB), block(KB), block(8)],
        out_shape=[shape(rows)] * 4 + [shape(KB), shape(KB), shape(8, F32)],
        scratch_shapes=[pltpu.VMEM((2, HALO + rows, LANES), F32)],
        compiler_params=params(),
        cost_estimate=pl.CostEstimate(flops=50_000_000, bytes_accessed=6_000_000, transcendentals=0),
        interpret=interpret,
        name="featurize",
    )(q, k, v, g, before, taps)


def toeplitz_kernel(taps, after, tc, ta):
    del after
    both = taps[...].reshape(16, LANES)
    row = lax.broadcasted_iota(jnp.int32, (LANES, LANES), 0)
    col = lax.broadcasted_iota(jnp.int32, (LANES, LANES), 1)
    flip = (row + col == LANES - 1).astype(BF16)
    turned = jnp.dot(both, flip, preferred_element_type=F32)
    straight = both.astype(F32)
    nothing = jnp.zeros((8, LANES), F32)
    for g in range(GPB):
        at = g // 4 * 8 + g % 4
        for out, lines, first in ((tc, turned, 1), (ta, straight, 0)):
            line = jnp.concatenate([jnp.broadcast_to(lines[at : at + 1], (8, LANES)), nothing], 1)
            base = pltpu.roll(line, first, 1, stride=1, stride_axis=0)
            for a in range(KB // 16):
                low = pltpu.roll(base, 16 * a, 1) if a else base
                high = pltpu.roll(base, 16 * a + 8, 1)
                out[g * KB + 16 * a : g * KB + 16 * a + 16] = jnp.concatenate([low, high], 0).astype(BF16)


def toeplitz(taps, after, interpret=False):
    blocks = taps.shape[0] // 2
    out = jax.ShapeDtypeStruct((blocks * GPB * KB, 2 * KB), BF16)
    return pl.pallas_call(
        toeplitz_kernel,
        grid=(blocks,),
        in_specs=[
            pl.BlockSpec((2, 8, LANES), lambda i: (i, 0, 0)),
            pl.BlockSpec((8, LANES), lambda i: (0, 0)),
        ],
        out_specs=[pl.BlockSpec((GPB * KB, 2 * KB), lambda i: (i, 0))] * 2,
        out_shape=[out, out],
        compiler_params=params(),
        cost_estimate=pl.CostEstimate(flops=50_000_000, bytes_accessed=17_000_000, transcendentals=0),
        interpret=interpret,
        name="toeplitz",
    )(taps, after)


def pick_groups(stacked, rows, start, count):
    groups = lane_group((count, LANES))
    out = stacked[start : start + count]
    for g in range(1, GPB):
        out = jnp.where(groups == g, stacked[g * rows + start : g * rows + start + count], out)
    return out


def align_left(tile):
    width = tile.shape[1]
    row = lax.broadcasted_iota(jnp.int32, tile.shape, 0)
    for bit in (1, 2, 4):
        tile = jnp.where(row // bit % 2 == 1, pltpu.roll(tile, width - bit, 1), tile)
    return tile


def inner_kernel(
    u, u_halo, d, d_halo, kf, vf, g, q, k, v, before, hexp, tc, ta,
    dq, dk, dv, up, part, pad, medium, grid_prod, last_prod,
):
    rows = u.shape[0]
    body = rows - 8
    uw = jnp.concatenate([u_halo[...].astype(F32), u[...].astype(F32)], 0)
    dw = jnp.concatenate([d[...].astype(F32), d_halo[...].astype(F32)], 0)
    u_low, u_high = uw[: 2 * KB].astype(BF16), uw[8:].astype(BF16)
    d_low, d_high = dw[: 2 * KB].astype(BF16), dw[8:].astype(BF16)

    grid_prod[:, :LANES] = jnp.dot(tc[...], u_low, preferred_element_type=F32)
    z_low = pick_groups(grid_prod.at[:, :LANES], KB, 0, KB)
    tails = jnp.concatenate([tc[i * KB + KB - 16 : (i + 1) * KB] for i in range(GPB)], 0)
    z_high = pick_groups(jnp.dot(tails, u_high, preferred_element_type=F32), 16, 8, 8)
    z = jnp.concatenate([z_low, z_high], 0)
    dq_feat = (g[...].astype(F32) * z).astype(BF16)

    grid_prod[:, LANES:] = jnp.dot(ta[...], d_high, preferred_element_type=F32)
    du_high = pick_groups(grid_prod.at[:, LANES:], KB, 0, KB)
    heads = jnp.concatenate([ta[i * KB : i * KB + 16] for i in range(GPB)], 0)
    du_low = pick_groups(jnp.dot(heads, d_low, preferred_element_type=F32), 16, 0, 8)
    du = jnp.concatenate([du_low, du_high], 0)
    dk_feat = (du * vf[...].astype(F32)).astype(BF16)
    dv_feat = (du * kf[...].astype(F32)).astype(BF16)

    sums = [jnp.zeros((1, LANES), F32)] * 8
    early = before[...].astype(F32)
    first = []
    for i, (x, feat, out) in enumerate(((q, dq_feat, dq), (k, dk_feat, dk), (v, dv_feat, dv))):
        out[...] = feat
        wide = feat.astype(F32)
        first.append(wide[:8])
        load_rows(pad, early[8 * i : 8 * i + 8], x[...].astype(F32))
        for j in range(KS):
            sums[j] = sums[j] + jnp.sum(wide * pad[HALO - j : HALO - j + rows], 0, keepdims=True)
    up[...] = jnp.concatenate(first, 0).astype(BF16)
    short = jnp.concatenate(sums + [jnp.zeros((LANES - 8, LANES), F32)], 0)
    gather = (lane_group((8, LANES)) == lax.broadcasted_iota(jnp.int32, (8, LANES), 0)).astype(F32)
    short = lax.dot_general(
        gather, short, (((1,), (1,)), ((), ())), precision=lax.Precision.HIGHEST,
        preferred_element_type=F32,
    )

    dv32 = dw[:rows]
    groups = lane_group((rows, LANES))
    masked = [jnp.where(groups == i, dv32, 0.0) for i in range(GPB)]
    contract = (((1,), (1,)), ((), ()))
    grid_prod[...] = lax.dot_general(
        jnp.concatenate([m[:body] for m in masked], 0).astype(BF16), u_low, contract,
        preferred_element_type=F32,
    )
    last_prod[...] = lax.dot_general(
        jnp.concatenate([m[body:] for m in masked], 0).astype(BF16), u_high, contract,
        preferred_element_type=F32,
    )
    for i in range(GPB):
        total = grid_prod[i * KB : i * KB + 8]
        for a in range(1, KB // 8):
            tile = grid_prod[i * KB + 8 * a : i * KB + 8 * a + 8]
            if a == KB // 8 - 1:
                tile = tile + last_prod[8 * i : 8 * i + 8]
            total = total + pltpu.roll(tile, 2 * KB - 8 * a, 1)
        line = jnp.sum(align_left(total), 0, keepdims=True)
        medium[i : i + 1] = pltpu.roll(line, 2 * KB - 1, 1)[:, :LANES]
    for half in range(2):
        part[half, 0:4] = medium[4 * half : 4 * half + 4]
        part[half, 4:8] = short[4 * half : 4 * half + 4]


def inner(u, u_halo, d, d_halo, kf, vf, g, q, k, v, before, hexp, tc, ta, interpret=False):
    rows, channels = u.shape
    blocks = channels // LANES
    block = lambda r: pl.BlockSpec((r, LANES), lambda i: (0, i))
    square = pl.BlockSpec((GPB * KB, 2 * KB), lambda i: (i, 0))
    shape = lambda r: jax.ShapeDtypeStruct((r, channels), BF16)
    return pl.pallas_call(
        inner_kernel,
        grid=(blocks,),
        in_specs=[block(rows), block(KB), block(rows), block(KB)]
        + [block(rows)] * 6
        + [block(24), block(8), square, square],
        out_specs=[block(rows)] * 3 + [block(24), pl.BlockSpec((2, 8, LANES), lambda i: (i, 0, 0))],
        out_shape=[shape(rows)] * 3
        + [shape(24), jax.ShapeDtypeStruct((2 * blocks, 8, LANES), F32)],
        scratch_shapes=[
            pltpu.VMEM((HALO + rows, LANES), F32),
            pltpu.VMEM((GPB, LANES), F32),
            pltpu.VMEM((GPB * KB, 2 * KB), F32),
            pltpu.VMEM((GPB * 8, 2 * KB), F32),
        ],
        compiler_params=params(),
        cost_estimate=pl.CostEstimate(flops=3_000_000_000, bytes_accessed=25_000_000, transcendentals=0),
        interpret=interpret,
        name="inner",
    )(u, u_halo, d, d_halo, kf, vf, g, q, k, v, before, hexp, tc, ta)


def project_kernel(dq, dk, dv, after, hexp, gq, gk, gv, pad):
    rows = dq.shape[0]
    for b in range(dq.shape[1] // LANES):
        lanes = slice(b * LANES, (b + 1) * LANES)
        h = hexp[:, lanes]
        late = after[:, lanes].astype(F32)
        for i, (x, out) in enumerate(((dq, gq), (dk, gk), (dv, gv))):
            slot = pad.at[(3 * b + i) % 2]
            load_rows(slot, x[:, lanes].astype(F32), late[8 * i : 8 * i + 8])
            total = h[0:1] * slot[0:rows]
            for j in range(1, KS):
                total = total + h[j : j + 1] * slot[j : j + rows]
            out[:, lanes] = total.astype(BF16)


def project(dq, dk, dv, after, hexp, interpret=False):
    rows, channels = dq.shape
    wide = 512
    block = lambda r: pl.BlockSpec((r, wide), lambda i: (0, i))
    return pl.pallas_call(
        project_kernel,
        grid=(channels // wide,),
        in_specs=[block(rows)] * 3 + [block(24), block(8)],
        out_specs=[block(rows)] * 3,
        out_shape=[jax.ShapeDtypeStruct((rows, channels), BF16)] * 3,
        scratch_shapes=[pltpu.VMEM((2, rows + HALO, LANES), F32)],
        compiler_params=params(),
        cost_estimate=pl.CostEstimate(flops=30_000_000, bytes_accessed=4_000_000, transcendentals=0),
        interpret=interpret,
        name="project",
    )(dq, dk, dv, after, hexp)


def step_ctx(value, step):
    count = lax.axis_size(CTX)
    return lax.ppermute(value, CTX, [(i, i + step) for i in range(count) if 0 <= i + step < count])


def swap_x_mp(value):
    nx, nz, ny, nm = SIZES
    at = lambda x, z, y, m: ((x * nz + z) * ny + y) * nm + m
    pairs = [
        (at(x, z, y, m), at(m, z, y, x))
        for x in range(nx) for z in range(nz) for y in range(ny) for m in range(nm)
    ]
    return lax.ppermute(value, ALL, pairs)


def pack_taps(filt_short, filt_medium):
    short = jnp.pad(filt_short.T, ((0, 0), (0, LANES - KS)))
    return jnp.concatenate([filt_medium.T, short], 0)


def shards(q, k, v, g, filt_short, filt_medium):
    rows = q.shape[0]
    tails = jnp.concatenate([x[rows - HALO :] for x in (q, k, v)], 0)
    before = step_ctx(tails, 1)
    own = swap_x_mp(pack_taps(filt_short, filt_medium))
    taps = lax.all_to_all(
        jnp.broadcast_to(own[None], (32, 8, LANES)), ("z", "yh"), 0, 0, tiled=True
    )
    u, d, kf, vf, u_send, d_send, hexp = featurize(q, k, v, g, before, taps)
    u_halo = step_ctx(u_send, 1)
    d_halo = step_ctx(d_send, -1)
    tc, ta = toeplitz(taps, hexp)
    dq, dk, dv, up, part = inner(u, u_halo, d, d_halo, kf, vf, g, q, k, v, before, hexp, tc, ta)
    after = step_ctx(up, -1)
    pieces = lax.all_to_all(part, ("z", "yh"), 0, 0, tiled=True)
    total = lax.psum(swap_x_mp(jnp.sum(pieces, 0)), MP)
    grad_q, grad_k, grad_v = project(dq, dk, dv, after, hexp)
    return grad_q, grad_k, grad_v, total[4:8, :KS].T, total[0:4, ::-1].T


def solution(mesh):
    fine = Mesh(mesh.devices.reshape(4, 8, 4, 2, 2), ALL)
    signal = P(CTX, MP)
    taps = P(None, CTX)
    return jax.shard_map(
        shards,
        mesh=fine,
        in_specs=(signal,) * 4 + (taps,) * 2,
        out_specs=(signal,) * 3 + (taps,) * 2,
        check_vma=False,
    )
```

```python
import jax
import jax.numpy as jnp
from jax import lax
from jax.experimental import pallas as pl
from jax.experimental.pallas import tpu as pltpu
from jax.sharding import Mesh, PartitionSpec as P

F32 = jnp.float32
BF16 = jnp.bfloat16
CPG = 16
KS = 7
KB = 128
LANES = 128
GPB = LANES // CPG
HALO = 8
CTX = ("x", "z", "yh")
MP = ("yl", "core")
ALL = CTX + MP
SIZES = (4, 8, 4, 4)
VMEM = 56 * 1024 * 1024


def params(**more):
    return pltpu.CompilerParams(vmem_limit_bytes=VMEM, **more)


def lane_group(shape):
    return lax.broadcasted_iota(jnp.int32, shape, len(shape) - 1) // CPG


def short_taps(taps):
    row = lax.broadcasted_iota(jnp.int32, (16, LANES), 0)
    group = jnp.where(row % 8 >= 4, row // 8 * 4 + row % 4, -1)
    spread = (lane_group((16, LANES)) == group).astype(F32)
    return lax.dot_general(
        taps[:, :LANES].T, spread, (((1,), (0,)), ((), ())), precision=lax.Precision.HIGHEST,
        preferred_element_type=F32,
    )[:8]


def fused_kernel(
    q, k, v, g, below, above, taps, gq, gk, gv, part,
    qs, ks, vs, feats, tc, ta, prod, last, medium,
):
    rows = q.shape[0]
    near = rows + 8
    lane = lax.broadcasted_iota(jnp.int32, (16, LANES), 1)
    row = lax.broadcasted_iota(jnp.int32, (16, LANES), 0)
    both = taps[...].reshape(16, LANES)
    straight = both.astype(F32)
    h = short_taps(straight)

    at = lax.broadcasted_iota(jnp.int32, (LANES, LANES), 0)
    to = lax.broadcasted_iota(jnp.int32, (LANES, LANES), 1)
    flip = (at + to == LANES - 1).astype(BF16)
    turned = jnp.dot(both, flip, preferred_element_type=F32)
    for i in range(GPB):
        line = i // 4 * 8 + i % 4
        for out, lines, first in ((tc, turned, 1), (ta, straight, 0)):
            base = pltpu.roll(
                jnp.broadcast_to(lines[line : line + 1], (16, LANES)), first, 1, stride=1, stride_axis=0
            )
            for a in range(KB // 16):
                tile = pltpu.roll(base, 16 * a, 1) if a else base
                if first:
                    upper = lane > row + 16 * a
                else:
                    upper = lane >= row + 16 * a
                place = slice(i * KB + 16 * a, i * KB + 16 * a + 16)
                out[place, :KB] = jnp.where(upper, tile, 0.0).astype(BF16)
                out[place, KB:] = jnp.where(upper, 0.0, tile).astype(BF16)

    early, late = below[...].astype(F32), above[...].astype(F32)
    ks[0:rows] = early[:rows]
    ks[rows : 2 * rows] = k[...].astype(F32)
    ks[2 * rows : 2 * rows + 8] = late[2 * rows : 2 * rows + 8]
    vs[0:rows] = early[rows : 2 * rows]
    vs[rows : 2 * rows] = v[...].astype(F32)
    vs[2 * rows : 2 * rows + 8] = late[2 * rows + 8 :]
    qs[0:8] = early[2 * rows + 8 :]
    qs[8 : rows + 8] = q[...].astype(F32)
    qs[rows + 8 : 2 * rows + 8] = late[:rows]

    def causal(slot):
        count = 2 * rows
        total = h[0:1] * slot[8 : 8 + count]
        for j in range(1, KS):
            total = total + h[j : j + 1] * slot[8 - j : 8 - j + count]
        return total.astype(BF16)

    kf, vf, qf = causal(ks), causal(vs), causal(qs)
    gate = jnp.concatenate([g[...].astype(F32), late[rows : 2 * rows]], 0)
    uw = kf.astype(F32) * vf.astype(F32)
    dw = gate * qf.astype(F32)
    u_low, u_high = uw[: 2 * KB].astype(BF16), uw[16:].astype(BF16)
    d_low, d_high = dw[: 2 * KB].astype(BF16), dw[16:].astype(BF16)

    prod[:, :LANES] = jnp.dot(tc[...], u_low, preferred_element_type=F32)
    z_low = pick_groups(prod.at[:, :LANES], KB, 0, KB)
    tails = jnp.concatenate([tc[(i + 1) * KB - 16 : (i + 1) * KB] for i in range(GPB)], 0)
    z_high = pick_groups(jnp.dot(tails, u_high, preferred_element_type=F32), 16, 0, 16)
    z = jnp.concatenate([z_low, z_high], 0)
    feats[0] = (gate[:near] * z).astype(BF16).astype(F32)

    prod[:, LANES:] = jnp.dot(ta[...], d_high, preferred_element_type=F32)
    du_high = pick_groups(prod.at[:, LANES:], KB, 0, KB)
    heads = jnp.concatenate([ta[i * KB : i * KB + 16] for i in range(GPB)], 0)
    du_low = pick_groups(jnp.dot(heads, d_low, preferred_element_type=F32), 16, 0, 16)
    du = jnp.concatenate([du_low, du_high], 0)
    feats[1] = (du * vf[KB:].astype(F32)).astype(BF16).astype(F32)
    feats[2] = (du * kf[KB:].astype(F32)).astype(BF16).astype(F32)

    sums = [jnp.zeros((1, LANES), F32)] * 8
    for i, (slot, base, out) in enumerate(((qs, 8, gq), (ks, rows, gk), (vs, rows, gv))):
        wide = feats[i, 0:rows]
        for j in range(KS):
            sums[j] = sums[j] + jnp.sum(wide * slot[base - j : base - j + rows], 0, keepdims=True)
        total = h[0:1] * wide
        for j in range(1, KS):
            total = total + h[j : j + 1] * feats[i, j : j + rows]
        out[...] = total.astype(BF16)
    short = jnp.concatenate(sums + [jnp.zeros((LANES - 8, LANES), F32)], 0)
    gather = (lane_group((8, LANES)) == lax.broadcasted_iota(jnp.int32, (8, LANES), 0)).astype(F32)
    short = lax.dot_general(
        gather, short, (((1,), (1,)), ((), ())), precision=lax.Precision.HIGHEST,
        preferred_element_type=F32,
    )

    own = jnp.concatenate([dw[:rows], jnp.zeros((8, LANES), F32)], 0)
    groups = lane_group((near, LANES))
    masked = [jnp.where(groups == i, own, 0.0) for i in range(GPB)]
    contract = (((1,), (1,)), ((), ()))
    prod[...] = lax.dot_general(
        jnp.concatenate([m[:KB] for m in masked], 0).astype(BF16), u_low, contract,
        preferred_element_type=F32,
    )
    last[...] = lax.dot_general(
        jnp.concatenate([m[KB:] for m in masked], 0).astype(BF16), u_high, contract,
        preferred_element_type=F32,
    )
    lane8, row8 = lane[:8], row[:8]
    for i in range(GPB):
        total = None
        for a in range(KB // 8):
            tile = prod[i * KB + 8 * a : i * KB + 8 * a + 8]
            if a == KB // 8 - 2:
                tile = tile + last[16 * i : 16 * i + 8]
            tile = jnp.where(lane8 > row8 + 8 * a, tile[:, :KB], tile[:, KB:])
            total = tile if a == 0 else total + pltpu.roll(tile, KB - 8 * a, 1)
        line = jnp.sum(align_left(total), 0, keepdims=True)
        medium[i : i + 1] = pltpu.roll(line, KB - 1, 1)
    ahead = jnp.dot(
        medium[...], flip.astype(F32), precision=lax.Precision.HIGHEST, preferred_element_type=F32
    )
    for half in range(2):
        part[half, 0:4] = ahead[4 * half : 4 * half + 4]
        part[half, 4:8] = short[4 * half : 4 * half + 4]


def fused(q, k, v, g, below, above, taps, interpret=False):
    rows, channels = q.shape
    blocks = channels // LANES
    block = lambda r: pl.BlockSpec((r, LANES), lambda i: (0, i))
    chunk = pl.BlockSpec((2, 8, LANES), lambda i: (i, 0, 0))
    return pl.pallas_call(
        fused_kernel,
        grid=(blocks,),
        in_specs=[block(rows)] * 4 + [block(2 * rows + 16)] * 2 + [chunk],
        out_specs=[block(rows)] * 3 + [chunk],
        out_shape=[jax.ShapeDtypeStruct((rows, channels), BF16)] * 3
        + [jax.ShapeDtypeStruct((2 * blocks, 8, LANES), F32)],
        scratch_shapes=[pltpu.VMEM((2 * rows + 8, LANES), F32)] * 3
        + [
            pltpu.VMEM((3, rows + 8, LANES), F32),
            pltpu.VMEM((GPB * KB, 2 * KB), BF16),
            pltpu.VMEM((GPB * KB, 2 * KB), BF16),
            pltpu.VMEM((GPB * KB, 2 * KB), F32),
            pltpu.VMEM((GPB * 16, 2 * KB), F32),
            pltpu.VMEM((GPB, LANES), F32),
        ],
        compiler_params=params(),
        cost_estimate=pl.CostEstimate(flops=4_000_000_000, bytes_accessed=10_000_000, transcendentals=0),
        interpret=interpret,
        name="fused",
    )(q, k, v, g, below, above, taps)


def pick_groups(stacked, rows, start, count):
    groups = lane_group((count, LANES))
    out = stacked[start : start + count]
    for g in range(1, GPB):
        out = jnp.where(groups == g, stacked[g * rows + start : g * rows + start + count], out)
    return out


def align_left(tile):
    width = tile.shape[1]
    row = lax.broadcasted_iota(jnp.int32, tile.shape, 0)
    for bit in (1, 2, 4):
        tile = jnp.where(row // bit % 2 == 1, pltpu.roll(tile, width - bit, 1), tile)
    return tile


def step_ctx(value, step):
    count = lax.axis_size(CTX)
    return lax.ppermute(value, CTX, [(i, i + step) for i in range(count) if 0 <= i + step < count])


def swap_x_mp(value):
    nx, nz, ny, nm = SIZES
    at = lambda x, z, y, m: ((x * nz + z) * ny + y) * nm + m
    pairs = [
        (at(x, z, y, m), at(m, z, y, x))
        for x in range(nx) for z in range(nz) for y in range(ny) for m in range(nm)
    ]
    return lax.ppermute(value, ALL, pairs)


def pack_taps(filt_short, filt_medium):
    short = jnp.pad(filt_short.T, ((0, 0), (0, LANES - KS)))
    return jnp.concatenate([filt_medium.T, short], 0)


def shards(q, k, v, g, filt_short, filt_medium):
    rows = q.shape[0]
    own, lower, upper = lax.optimization_barrier((
        swap_x_mp(pack_taps(filt_short, filt_medium)),
        jnp.concatenate([k, v, q[rows - 16 :]], 0),
        jnp.concatenate([q, g, k[:8], v[:8]], 0),
    ))
    below, above = step_ctx(lower, 1), step_ctx(upper, -1)
    taps = lax.all_to_all(
        jnp.broadcast_to(own[None], (32, 8, LANES)), ("z", "yh"), 0, 0, tiled=True
    )
    grad_q, grad_k, grad_v, part = fused(q, k, v, g, below, above, taps)
    pieces = lax.all_to_all(part, ("z", "yh"), 0, 0, tiled=True)
    total = lax.psum(swap_x_mp(jnp.sum(pieces, 0)), MP)
    return grad_q, grad_k, grad_v, total[4:8, :KS].T, total[0:4].T


def solution(mesh):
    fine = Mesh(mesh.devices.reshape(4, 8, 4, 2, 2), ALL)
    signal = P(CTX, MP)
    taps = P(None, CTX)
    return jax.shard_map(
        shards,
        mesh=fine,
        in_specs=(signal,) * 4 + (taps,) * 2,
        out_specs=(signal,) * 3 + (taps,) * 2,
        check_vma=False,
    )
```

```python
import functools

import jax
import jax.numpy as jnp
from jax import lax
from jax.experimental import pallas as pl
from jax.experimental.pallas import tpu as pltpu
from jax.sharding import Mesh, PartitionSpec as P

F32 = jnp.float32
BF16 = jnp.bfloat16
CPG = 16
KS = 7
KB = 128
LANES = 128
GPB = LANES // CPG
HALO = 8
CTX = ("x", "z", "yh")
MP = ("yl", "core")
ALL = CTX + MP
SIZES = (4, 8, 4, 4)
VMEM = 12 * 1024 * 1024


def params(**more):
    return pltpu.CompilerParams(vmem_limit_bytes=VMEM, **more)


def lane_group(shape):
    return lax.broadcasted_iota(jnp.int32, shape, len(shape) - 1) // CPG


def short_taps(taps):
    row = lax.broadcasted_iota(jnp.int32, (16, LANES), 0)
    group = jnp.where(row % 8 >= 4, row // 8 * 4 + row % 4, -1)
    spread = (lane_group((16, LANES)) == group).astype(BF16)
    return lax.dot_general(taps, spread, (((0,), (0,)), ((), ())), preferred_element_type=F32)[:8]


def fused_kernel(raw, q, k, v, g, below, above, extra, taps, *rest_refs):
    gq, gk, gv, part, qs, ks, vs, feats = rest_refs[-8:]
    rows = q.shape[0]
    near = rows + 8
    both = taps[...].reshape(16, LANES)
    h = short_taps(both)

    def causal(slot, count):
        total = h[0:1] * slot[8 : 8 + count]
        for j in range(1, KS):
            total = total + h[j : j + 1] * slot[8 - j : 8 - j + count]
        return total.astype(BF16).astype(F32)

    early, late = below[...].astype(F32), above[...].astype(F32)
    if raw:
        ks[0:rows] = early[:rows]
        ks[rows : 2 * rows] = k[...].astype(F32)
        ks[2 * rows : 2 * rows + 8] = late[2 * rows : 2 * rows + 8]
        vs[0:rows] = early[rows : 2 * rows]
        vs[rows : 2 * rows] = v[...].astype(F32)
        vs[2 * rows : 2 * rows + 8] = late[2 * rows + 8 :]
        qs[0:8] = early[2 * rows + 8 :]
        qs[8 : rows + 8] = q[...].astype(F32)
        qs[rows + 8 : 2 * rows + 8] = late[:rows]
        kf, vf, qf = (causal(x, 2 * rows) for x in (ks, vs, qs))
        gate = jnp.concatenate([g[...].astype(F32), late[rows : 2 * rows]], 0)
        uw = kf * vf
        dw = gate * qf
        kf, vf = kf[KB:], vf[KB:]
        own_at = rows
    else:
        tails = extra[...].astype(F32)
        for i, (slot, x) in enumerate(((ks, k), (vs, v), (qs, q))):
            slot[0:8] = tails[16 * i + 8 : 16 * i + 16]
            slot[8 : rows + 8] = x[...].astype(F32)
        kf, vf, qf = (causal(x, rows) for x in (ks, vs, qs))
        gate = jnp.concatenate([g[...].astype(F32), late[rows : rows + 8]], 0)
        kf = jnp.concatenate([kf, late[rows + 8 : rows + 16]], 0)
        vf = jnp.concatenate([vf, late[rows + 16 :]], 0)
        uw = jnp.concatenate([early, kf * vf], 0)
        dw = jnp.concatenate([gate[:rows] * qf, late[:rows]], 0)
        own_at = 8
    u_low, u_high = uw[: 2 * KB].astype(BF16), uw[16:].astype(BF16)
    d_low, d_high = dw[: 2 * KB].astype(BF16), dw[16:].astype(BF16)
    own = jnp.concatenate([dw[:rows], jnp.zeros((8, LANES), F32)], 0).astype(BF16)

    at = lax.broadcasted_iota(jnp.int32, (LANES, LANES), 0)
    to = lax.broadcasted_iota(jnp.int32, (LANES, LANES), 1)
    flip = (at + to == LANES - 1).astype(BF16)
    straight = both.astype(F32)
    turned = jnp.dot(both, flip, preferred_element_type=F32)
    lane = lax.broadcasted_iota(jnp.int32, (16, LANES), 1)
    row = lax.broadcasted_iota(jnp.int32, (16, LANES), 0)
    lane8, row8 = lane[:8], row[:8]
    contract = (((1,), (1,)), ((), ()))
    wide = lane_group((2 * KB, LANES))

    def square(line, first):
        base = pltpu.roll(jnp.broadcast_to(line, (16, LANES)), first, 1, stride=1, stride_axis=0)
        tiles = []
        for a in range(KB // 16):
            tile = pltpu.roll(base, 16 * a, 1) if a else base
            upper = lane > row + 16 * a if first else lane >= row + 16 * a
            parts = [jnp.where(upper, tile, 0.0), jnp.where(upper, 0.0, tile)]
            tiles.append(jnp.concatenate(parts, 1).astype(BF16))
        return tiles

    z_low = du_high = jnp.zeros((KB, LANES), F32)
    tails, heads, medium = [], [], []
    rest = jnp.concatenate([jnp.where(wide[:16] == i, own[KB:], 0) for i in range(GPB)], 0)
    last = lax.dot_general(rest, u_high, contract, preferred_element_type=F32)
    for i in range(GPB):
        line = i // 4 * 8 + i % 4
        tc = square(turned[line : line + 1], 1)
        ta = square(straight[line : line + 1], 0)
        tails.append(tc[-1])
        heads.append(ta[0])
        z_low = z_low + jnp.dot(
            jnp.concatenate(tc, 0), jnp.where(wide == i, u_low, 0), preferred_element_type=F32
        )
        du_high = du_high + jnp.dot(
            jnp.concatenate(ta, 0), jnp.where(wide == i, d_high, 0), preferred_element_type=F32
        )
        mine = jnp.where(wide[:KB] == i, own[:KB], 0)
        prod = lax.dot_general(mine, u_low, contract, preferred_element_type=F32)
        total = None
        for a in range(KB // 8):
            tile = prod[8 * a : 8 * a + 8]
            if a == KB // 8 - 2:
                tile = tile + last[16 * i : 16 * i + 8]
            tile = jnp.where(lane8 > row8 + 8 * a, tile[:, :KB], tile[:, KB:])
            total = tile if a == 0 else total + pltpu.roll(tile, KB - 8 * a, 1)
        medium.append(jnp.sum(align_left(total), 0, keepdims=True))
    for half in range(2):
        part[half, 0, 0:4] = jnp.concatenate(medium[4 * half : 4 * half + 4], 0)

    z_high = pick_groups(
        jnp.dot(jnp.concatenate(tails, 0), u_high, preferred_element_type=F32), 16, 0, 16
    )
    du_low = pick_groups(
        jnp.dot(jnp.concatenate(heads, 0), d_low, preferred_element_type=F32), 16, 0, 16
    )
    z = jnp.concatenate([z_low, z_high], 0)
    du = jnp.concatenate([du_low, du_high], 0)
    feats[0] = (gate[:near] * z).astype(BF16).astype(F32)
    feats[1] = (du * vf).astype(BF16).astype(F32)
    feats[2] = (du * kf).astype(BF16).astype(F32)

    sums = [jnp.zeros((8, LANES), F32)] * 8
    for i, (slot, base, out) in enumerate(((qs, 8, gq), (ks, own_at, gk), (vs, own_at, gv))):
        wide_feat = feats[i, 0:rows]
        for j in range(KS):
            both_rows = wide_feat * slot[base - j : base - j + rows]
            sums[j] = sums[j] + jnp.sum(both_rows.reshape(rows // 8, 8, LANES), 0)
        total = h[0:1] * wide_feat
        for j in range(1, KS):
            total = total + h[j : j + 1] * feats[i, j : j + rows]
        out[...] = total.astype(BF16)
    short = jnp.concatenate([jnp.sum(x, 0, keepdims=True) for x in sums], 0)
    swapped = pltpu.roll(short, LANES // 2, 1)
    left = lane[:4] < LANES // 2
    part[0, 0, 4:8] = jnp.where(left, short[:4], swapped[4:])
    part[1, 0, 4:8] = jnp.where(left, swapped[:4], short[4:])


def fused(raw, q, k, v, g, below, above, extra, taps, first, count, written=None, interpret=False):
    rows, channels = q.shape
    every = channels // LANES
    block = lambda r: pl.BlockSpec((r, LANES), lambda i: (0, first + i))
    chunk = pl.BlockSpec((2, 1, 8, LANES), lambda i: ((first + i) % 2, (first + i) // 2, 0, 0))
    written = () if written is None else tuple(written)
    depth = 2 * rows + 8 if raw else rows + 8
    return pl.pallas_call(
        functools.partial(fused_kernel, raw),
        grid=(count,),
        in_specs=[block(rows)] * 4
        + [
            pl.BlockSpec((2 * rows + 16 if raw else KB, LANES), lambda i: (0, i)),
            pl.BlockSpec((2 * rows + 16 if raw else rows + 24, LANES), lambda i: (0, i)),
            pl.BlockSpec((48, LANES), lambda i: (0, i)),
            chunk,
        ]
        + [pl.BlockSpec(memory_space=pl.ANY)] * len(written),
        out_specs=[block(rows)] * 3 + [chunk],
        out_shape=[jax.ShapeDtypeStruct((rows, channels), BF16)] * 3
        + [jax.ShapeDtypeStruct((4, every // 2, 8, LANES), F32)],
        scratch_shapes=[pltpu.VMEM((depth, LANES), F32)] * 3
        + [pltpu.VMEM((3, rows + 8, LANES), F32)],
        input_output_aliases={8 + n: n for n in range(len(written))},
        compiler_params=params(),
        cost_estimate=pl.CostEstimate(
            flops=250_000_000 * count, bytes_accessed=500_000 * count, transcendentals=0
        ),
        interpret=interpret,
        name="fused_raw" if raw else "fused_sent",
    )(q, k, v, g, below, above, extra, taps, *written)


def pack_kernel(q, k, v, g, qb, kb, vb, lower, upper, tails):
    rows = q.shape[0]
    tail = lambda x: x[...].astype(F32)[rows - 16 :]
    lower[...] = jnp.concatenate(
        [k[...].astype(F32), v[...].astype(F32), tail(q)], 0
    ).astype(BF16)
    tails[...] = jnp.concatenate([tail(kb), tail(vb), tail(qb)], 0).astype(BF16)
    upper[...] = jnp.concatenate(
        [q[...].astype(F32), g[...].astype(F32), k[...].astype(F32)[:8], v[...].astype(F32)[:8]], 0
    ).astype(BF16)


def pack(q, k, v, g, split, interpret=False):
    rows, channels = q.shape
    wide = 256
    assert channels == 2 * split
    low = lambda r: pl.BlockSpec((r, wide), lambda i: (0, i))
    high = pl.BlockSpec((rows, wide), lambda i: (0, split // wide + i))
    return pl.pallas_call(
        pack_kernel,
        grid=(split // wide,),
        in_specs=[low(rows)] * 4 + [high] * 3,
        out_specs=[low(2 * rows + 16), low(2 * rows + 16), low(48)],
        out_shape=[
            jax.ShapeDtypeStruct((2 * rows + 16, split), BF16),
            jax.ShapeDtypeStruct((2 * rows + 16, split), BF16),
            jax.ShapeDtypeStruct((48, split), BF16),
        ],
        compiler_params=params(),
        interpret=interpret,
        name="pack",
    )(q, k, v, g, q, k, v)


def products_kernel(q, k, v, g, extra, taps, lower, upper, qs, ks, vs):
    rows = q.shape[0]
    h = short_taps(taps[...].reshape(16, LANES))
    tails = extra[...].astype(F32)
    made = []
    for i, (slot, x) in enumerate(((ks, k), (vs, v), (qs, q))):
        slot[0:8] = tails[16 * i + 8 : 16 * i + 16]
        slot[8 : rows + 8] = x[...].astype(F32)
        total = h[0:1] * slot[8 : 8 + rows]
        for j in range(1, KS):
            total = total + h[j : j + 1] * slot[8 - j : 8 - j + rows]
        made.append(total.astype(BF16).astype(F32))
    kf, vf, qf = made
    lower[...] = (kf * vf)[rows - KB :].astype(BF16)
    gate = g[...].astype(F32)
    upper[...] = jnp.concatenate([gate * qf, gate[:8], kf[:8], vf[:8]], 0).astype(BF16)


def products(q, k, v, g, extra, taps, split, interpret=False):
    rows, channels = q.shape
    first = split // LANES
    block = pl.BlockSpec((rows, LANES), lambda i: (0, first + i))
    out = lambda r: pl.BlockSpec((r, LANES), lambda i: (0, i))
    chunk = pl.BlockSpec((2, 1, 8, LANES), lambda i: ((first + i) % 2, (first + i) // 2, 0, 0))
    return pl.pallas_call(
        products_kernel,
        grid=((channels - split) // LANES,),
        in_specs=[block] * 4 + [pl.BlockSpec((48, LANES), lambda i: (0, i)), chunk],
        out_specs=[out(KB), out(rows + 24)],
        out_shape=[
            jax.ShapeDtypeStruct((KB, channels - split), BF16),
            jax.ShapeDtypeStruct((rows + 24, channels - split), BF16),
        ],
        scratch_shapes=[pltpu.VMEM((rows + 8, LANES), F32)] * 3,
        compiler_params=params(),
        cost_estimate=pl.CostEstimate(flops=20_000_000, bytes_accessed=3_000_000, transcendentals=0),
        interpret=interpret,
        name="products",
    )(q, k, v, g, extra, taps)


def pick_groups(stacked, rows, start, count):
    groups = lane_group((count, LANES))
    out = stacked[start : start + count]
    for g in range(1, GPB):
        out = jnp.where(groups == g, stacked[g * rows + start : g * rows + start + count], out)
    return out


def align_left(tile):
    width = tile.shape[1]
    row = lax.broadcasted_iota(jnp.int32, tile.shape, 0)
    for bit in (1, 2, 4):
        tile = jnp.where(row // bit % 2 == 1, pltpu.roll(tile, width - bit, 1), tile)
    return tile


def step_ctx(value, step):
    count = lax.axis_size(CTX)
    return lax.ppermute(value, CTX, [(i, i + step) for i in range(count) if 0 <= i + step < count])


def turn(value, back=False):
    nx, nz, ny, nm = SIZES
    at = lambda x, z, y, m: ((x * nz + z) * ny + y) * nm + m
    pairs = [
        (at(x, z, y, m), at(y, z, m, x))
        for x in range(nx) for z in range(nz) for y in range(ny) for m in range(nm)
    ]
    if back:
        pairs = [(b, a) for a, b in pairs]
    return lax.ppermute(value, ALL, pairs)


def pack_taps(filt_short, filt_medium):
    short = jnp.pad(filt_short.T, ((0, 0), (0, LANES - KS)))
    return jnp.concatenate([filt_medium.T, short], 0)


def shards(q, k, v, g, filt_short, filt_medium):
    rows, channels = q.shape
    split = channels // 2
    lower, upper, tails = pack(q, k, v, g, split)
    own, tails, lower, upper = lax.optimization_barrier(
        (turn(pack_taps(filt_short, filt_medium)), step_ctx(tails, 1), lower, upper)
    )
    below, above = step_ctx(lower, 1), step_ctx(upper, -1)
    taps = lax.all_to_all(
        jnp.broadcast_to(own[None], (32, 8, LANES)), ("x", "z"), 0, 0, tiled=True
    ).reshape(4, 8, 8, LANES)
    u_send, d_send = products(q, k, v, g, tails, taps, split)
    u_halo, d_halo = step_ctx(u_send, 1), step_ctx(d_send, -1)
    blocks = split // LANES
    made = fused(True, q, k, v, g, below, above, tails, taps, 0, blocks)
    made = fused(False, q, k, v, g, u_halo, d_halo, tails, taps, blocks, blocks, made)
    grad_q, grad_k, grad_v, part = made
    pieces = lax.all_to_all(part.reshape(32, 8, LANES), ("x", "z"), 0, 0, tiled=True)
    total = lax.psum(turn(jnp.sum(pieces, 0), back=True), MP)
    grad_short, grad_medium = finish(total)
    return grad_q, grad_k, grad_v, grad_short[:, :KS].T, grad_medium.T


def finish_kernel(total, short, medium):
    at = lax.broadcasted_iota(jnp.int32, (LANES, LANES), 0)
    to = lax.broadcasted_iota(jnp.int32, (LANES, LANES), 1)
    medium[...] = jnp.dot(
        total[0:4], ((at + to) % LANES == 0).astype(F32), precision=lax.Precision.HIGHEST,
        preferred_element_type=F32,
    )
    group = lax.broadcasted_iota(jnp.int32, (4, LANES), 0)
    for half in range(2):
        spread = (lane_group((4, LANES)) == group + 4 * half).astype(F32)
        short[:, 4 * half : 4 * half + 4] = lax.dot_general(
            spread, total[4:8], (((1,), (1,)), ((), ())), precision=lax.Precision.HIGHEST,
            preferred_element_type=F32,
        )


def finish(total, interpret=False):
    return pl.pallas_call(
        finish_kernel,
        out_shape=[jax.ShapeDtypeStruct((4, 8), F32), jax.ShapeDtypeStruct((4, LANES), F32)],
        interpret=interpret,
        name="finish",
    )(total)


def solution(mesh):
    fine = Mesh(mesh.devices.reshape(4, 8, 4, 2, 2), ALL)
    signal = P(CTX, MP)
    taps = P(None, CTX)
    return jax.shard_map(
        shards,
        mesh=fine,
        in_specs=(signal,) * 4 + (taps,) * 2,
        out_specs=(signal,) * 3 + (taps,) * 2,
        check_vma=False,
    )
```

```python
import functools

import jax
import jax.numpy as jnp
from jax import lax
from jax.experimental import pallas as pl
from jax.experimental.pallas import tpu as pltpu
from jax.sharding import Mesh, PartitionSpec as P

F32 = jnp.float32
BF16 = jnp.bfloat16
CPG = 16
KS = 7
KB = 128
LANES = 128
GPB = LANES // CPG
HALO = 8
CTX = ("x", "z", "yh")
MP = ("yl", "core")
ALL = CTX + MP
SIZES = (4, 8, 4, 4)
VMEM = 12 * 1024 * 1024


def params(**more):
    return pltpu.CompilerParams(vmem_limit_bytes=VMEM, **more)


def lane_group(shape):
    return lax.broadcasted_iota(jnp.int32, shape, len(shape) - 1) // CPG


def short_taps(taps):
    row = lax.broadcasted_iota(jnp.int32, (16, LANES), 0)
    group = jnp.where(row % 8 >= 4, row // 8 * 4 + row % 4, -1)
    spread = (lane_group((16, LANES)) == group).astype(BF16)
    return lax.dot_general(taps, spread, (((0,), (0,)), ((), ())), preferred_element_type=F32)[:8]


def fused_kernel(q, k, v, g, u_before, d_after, tails, heads, taps, *refs):
    gq, gk, gv, part, qs, ks, vs, feats = refs[-8:]
    rows = q.shape[0]
    near = rows + 8
    both = taps[...].reshape(16, LANES)
    h = short_taps(both)
    early, late = tails[...].astype(F32), heads[...].astype(F32)
    made = []
    for i, (slot, x) in enumerate(((ks, k), (vs, v), (qs, q))):
        slot[0:8] = early[16 * i : 16 * i + 8]
        slot[8 : near] = x[...].astype(F32)
        count = rows
        if i < 2:
            slot[near : near + 8] = late[16 * i : 16 * i + 8]
            count = near
        made.append(causal(h, slot, count))
    kf, vf, qf = made
    gate = jnp.concatenate([g[...].astype(F32), late[32:40]], 0)
    uw = jnp.concatenate([u_before[...].astype(F32), kf * vf], 0)
    dw = jnp.concatenate([gate[:rows] * qf, d_after[...].astype(F32)], 0)
    u_low, u_high = uw[: 2 * KB].astype(BF16), uw[16:].astype(BF16)
    d_low, d_high = dw[: 2 * KB].astype(BF16), dw[16:].astype(BF16)
    own = jnp.concatenate([dw[:rows], jnp.zeros((8, LANES), F32)], 0).astype(BF16)

    at = lax.broadcasted_iota(jnp.int32, (LANES, LANES), 0)
    to = lax.broadcasted_iota(jnp.int32, (LANES, LANES), 1)
    flip = (at + to == LANES - 1).astype(BF16)
    straight = both.astype(F32)
    turned = jnp.dot(both, flip, preferred_element_type=F32)
    lane = lax.broadcasted_iota(jnp.int32, (16, LANES), 1)
    row = lax.broadcasted_iota(jnp.int32, (16, LANES), 0)
    lane8, row8 = lane[:8], row[:8]
    contract = (((1,), (1,)), ((), ()))
    wide = lane_group((2 * KB, LANES))

    def square(line, first):
        base = pltpu.roll(jnp.broadcast_to(line, (16, LANES)), first, 1, stride=1, stride_axis=0)
        tiles = []
        for a in range(KB // 16):
            tile = pltpu.roll(base, 16 * a, 1) if a else base
            upper = lane > row + 16 * a if first else lane >= row + 16 * a
            parts = [jnp.where(upper, tile, 0.0), jnp.where(upper, 0.0, tile)]
            tiles.append(jnp.concatenate(parts, 1).astype(BF16))
        return tiles

    z_low = du_high = jnp.zeros((KB, LANES), F32)
    tails, heads, medium = [], [], []
    rest = jnp.concatenate([jnp.where(wide[:16] == i, own[KB:], 0) for i in range(GPB)], 0)
    last = lax.dot_general(rest, u_high, contract, preferred_element_type=F32)
    for i in range(GPB):
        line = i // 4 * 8 + i % 4
        tc = square(turned[line : line + 1], 1)
        ta = square(straight[line : line + 1], 0)
        tails.append(tc[-1])
        heads.append(ta[0])
        z_low = z_low + jnp.dot(
            jnp.concatenate(tc, 0), jnp.where(wide == i, u_low, 0), preferred_element_type=F32
        )
        du_high = du_high + jnp.dot(
            jnp.concatenate(ta, 0), jnp.where(wide == i, d_high, 0), preferred_element_type=F32
        )
        mine = jnp.where(wide[:KB] == i, own[:KB], 0)
        prod = lax.dot_general(mine, u_low, contract, preferred_element_type=F32)
        total = None
        for a in range(KB // 8):
            tile = prod[8 * a : 8 * a + 8]
            if a == KB // 8 - 2:
                tile = tile + last[16 * i : 16 * i + 8]
            tile = jnp.where(lane8 > row8 + 8 * a, tile[:, :KB], tile[:, KB:])
            total = tile if a == 0 else total + pltpu.roll(tile, KB - 8 * a, 1)
        medium.append(jnp.sum(align_left(total), 0, keepdims=True))
    for half in range(2):
        part[half, 0, 0:4] = jnp.concatenate(medium[4 * half : 4 * half + 4], 0)

    z_high = pick_groups(
        jnp.dot(jnp.concatenate(tails, 0), u_high, preferred_element_type=F32), 16, 0, 16
    )
    du_low = pick_groups(
        jnp.dot(jnp.concatenate(heads, 0), d_low, preferred_element_type=F32), 16, 0, 16
    )
    z = jnp.concatenate([z_low, z_high], 0)
    du = jnp.concatenate([du_low, du_high], 0)
    feats[0] = (gate[:near] * z).astype(BF16).astype(F32)
    feats[1] = (du * vf).astype(BF16).astype(F32)
    feats[2] = (du * kf).astype(BF16).astype(F32)

    sums = [jnp.zeros((8, LANES), F32)] * 8
    for i, (slot, base, out) in enumerate(((qs, 8, gq), (ks, 8, gk), (vs, 8, gv))):
        wide_feat = feats[i, 0:rows]
        for j in range(KS):
            both_rows = wide_feat * slot[base - j : base - j + rows]
            sums[j] = sums[j] + jnp.sum(both_rows.reshape(rows // 8, 8, LANES), 0)
        total = h[0:1] * wide_feat
        for j in range(1, KS):
            total = total + h[j : j + 1] * feats[i, j : j + rows]
        out[...] = total.astype(BF16)
    short = jnp.concatenate([jnp.sum(x, 0, keepdims=True) for x in sums], 0)
    swapped = pltpu.roll(short, LANES // 2, 1)
    left = lane[:4] < LANES // 2
    part[0, 0, 4:8] = jnp.where(left, short[:4], swapped[4:])
    part[1, 0, 4:8] = jnp.where(left, swapped[:4], short[4:])


def fused(q, k, v, g, u_before, d_after, tails, heads, taps, first, count, written=(), interpret=False):
    rows, channels = q.shape
    block = lambda r: pl.BlockSpec((r, LANES), lambda i: (0, first + i))
    sent = lambda r: pl.BlockSpec((r, LANES), lambda i: (0, i))
    chunk = pl.BlockSpec((2, 1, 8, LANES), lambda i: ((first + i) % 2, (first + i) // 2, 0, 0))
    return pl.pallas_call(
        fused_kernel,
        grid=(count,),
        in_specs=[block(rows)] * 4 + [sent(KB), sent(rows), block(48), block(48), chunk]
        + [pl.BlockSpec(memory_space=pl.ANY)] * len(written),
        out_specs=[block(rows)] * 3 + [chunk],
        out_shape=[jax.ShapeDtypeStruct((rows, channels), BF16)] * 3
        + [jax.ShapeDtypeStruct((4, channels // LANES // 2, 8, LANES), F32)],
        scratch_shapes=[pltpu.VMEM((rows + 16, LANES), F32)] * 3
        + [pltpu.VMEM((3, rows + 8, LANES), F32)],
        input_output_aliases={9 + n: n for n in range(len(written))},
        compiler_params=params(),
        cost_estimate=pl.CostEstimate(
            flops=250_000_000 * count, bytes_accessed=500_000 * count, transcendentals=0
        ),
        interpret=interpret,
        name="fused",
    )(q, k, v, g, u_before, d_after, tails, heads, taps, *written)


def causal(h, slot, count):
    total = h[0:1] * slot[8 : 8 + count]
    for j in range(1, KS):
        total = total + h[j : j + 1] * slot[8 - j : 8 - j + count]
    return total.astype(BF16).astype(F32)


def ends_kernel(qt, kt, vt, kh, vh, gh, tails, heads):
    for out, parts in ((tails, (kt, vt, qt)), (heads, (kh, vh, gh))):
        for i, x in enumerate(parts):
            out[16 * i : 16 * i + 16] = x[...]


def ends(q, k, v, g, interpret=False):
    rows, channels = q.shape
    wide = channels // 2
    tail = pl.BlockSpec((16, wide), lambda i: (rows // 16, i))
    head = pl.BlockSpec((16, wide), lambda i: (0, i))
    whole = pl.BlockSpec((48, wide), lambda i: (0, i))
    return pl.pallas_call(
        ends_kernel,
        grid=(2,),
        in_specs=[tail] * 3 + [head] * 3,
        out_specs=[whole] * 2,
        out_shape=[jax.ShapeDtypeStruct((48, channels), BF16)] * 2,
        compiler_params=pltpu.CompilerParams(vmem_limit_bytes=56 * 1024 * 1024),
        interpret=interpret,
        name="ends",
    )(q, k, v, k, v, g)


def products_kernel(q, k, v, g, tails, taps, lower, upper, qs, ks, vs):
    rows = q.shape[0]
    h = short_taps(taps[...].reshape(16, LANES))
    early = tails[...].astype(F32)
    made = []
    for i, (slot, x) in enumerate(((ks, k), (vs, v), (qs, q))):
        slot[0:8] = early[16 * i : 16 * i + 8]
        slot[8 : rows + 8] = x[...].astype(F32)
        made.append(causal(h, slot, rows))
    kf, vf, qf = made
    lower[...] = (kf * vf)[rows - KB :].astype(BF16)
    upper[...] = (g[...].astype(F32) * qf).astype(BF16)


def products(q, k, v, g, tails, taps, first, count, interpret=False):
    rows = q.shape[0]
    block = lambda r: pl.BlockSpec((r, LANES), lambda i: (0, first + i))
    chunk = pl.BlockSpec((2, 1, 8, LANES), lambda i: ((first + i) % 2, (first + i) // 2, 0, 0))
    out = lambda r: pl.BlockSpec((r, LANES), lambda i: (0, i))
    return pl.pallas_call(
        products_kernel,
        grid=(count,),
        in_specs=[block(rows)] * 4 + [block(48), chunk],
        out_specs=[out(KB), out(rows)],
        out_shape=[jax.ShapeDtypeStruct((r, count * LANES), BF16) for r in (KB, rows)],
        scratch_shapes=[pltpu.VMEM((rows + 8, LANES), F32)] * 3,
        compiler_params=params(),
        cost_estimate=pl.CostEstimate(flops=20_000_000, bytes_accessed=3_000_000, transcendentals=0),
        interpret=interpret,
        name="products",
    )(q, k, v, g, tails, taps)


def pick_groups(stacked, rows, start, count):
    groups = lane_group((count, LANES))
    out = stacked[start : start + count]
    for g in range(1, GPB):
        out = jnp.where(groups == g, stacked[g * rows + start : g * rows + start + count], out)
    return out


def align_left(tile):
    width = tile.shape[1]
    row = lax.broadcasted_iota(jnp.int32, tile.shape, 0)
    for bit in (1, 2, 4):
        tile = jnp.where(row // bit % 2 == 1, pltpu.roll(tile, width - bit, 1), tile)
    return tile


def step_ctx(value, step):
    count = lax.axis_size(CTX)
    return lax.ppermute(value, CTX, [(i, i + step) for i in range(count) if 0 <= i + step < count])


def turn(value, back=False):
    nx, nz, ny, nm = SIZES
    at = lambda x, z, y, m: ((x * nz + z) * ny + y) * nm + m
    pairs = [
        (at(x, z, y, m), at(y, z, m, x))
        for x in range(nx) for z in range(nz) for y in range(ny) for m in range(nm)
    ]
    if back:
        pairs = [(b, a) for a, b in pairs]
    return lax.ppermute(value, ALL, pairs)


def pack_taps(filt_short, filt_medium):
    short = jnp.pad(filt_short.T, ((0, 0), (0, LANES - KS)))
    return jnp.concatenate([filt_medium.T, short], 0)


def shards(q, k, v, g, filt_short, filt_medium):
    blocks = q.shape[1] // LANES
    packed, *signals = lax.optimization_barrier((pack_taps(filt_short, filt_medium), q, k, v, g))
    own = turn(packed)
    tails, heads = ends(*signals)
    own, tails, heads = lax.optimization_barrier((own, step_ctx(tails, 1), step_ctx(heads, -1)))
    taps = lax.all_to_all(
        jnp.broadcast_to(own[None], (32, 8, LANES)), ("x", "z"), 0, 0, tiled=True
    ).reshape(4, 8, 8, LANES)
    half = blocks // 2
    pieces = [(0, half), (half, blocks - half)]
    sent = []
    for first, count in pieces:
        lower, upper = products(q, k, v, g, tails, taps, first, count)
        sent.append((step_ctx(lower, 1), step_ctx(upper, -1)))
    made = ()
    for (first, count), (u_before, d_after) in zip(pieces, sent):
        made = fused(q, k, v, g, u_before, d_after, tails, heads, taps, first, count, made)
    grad_q, grad_k, grad_v, part = made
    parts = lax.all_to_all(part.reshape(32, 8, LANES), ("x", "z"), 0, 0, tiled=True)
    total = lax.psum(turn(jnp.sum(parts, 0), back=True), MP)
    grad_short, grad_medium = finish(total)
    return grad_q, grad_k, grad_v, grad_short.T, grad_medium.T


def finish_kernel(total, short, medium):
    at = lax.broadcasted_iota(jnp.int32, (LANES, LANES), 0)
    to = lax.broadcasted_iota(jnp.int32, (LANES, LANES), 1)
    medium[...] = jnp.dot(
        total[0:4], ((at + to) % LANES == 0).astype(F32), precision=lax.Precision.HIGHEST,
        preferred_element_type=F32,
    )
    group = lax.broadcasted_iota(jnp.int32, (4, LANES), 0)
    halves = []
    for half in range(2):
        spread = (lane_group((4, LANES)) == group + 4 * half).astype(F32)
        halves.append(
            lax.dot_general(
                spread, total[4:8], (((1,), (1,)), ((), ())), precision=lax.Precision.HIGHEST,
                preferred_element_type=F32,
            )
        )
    short[...] = jnp.concatenate(halves, 1)[:, :KS]


def finish(total, interpret=False):
    return pl.pallas_call(
        finish_kernel,
        out_shape=[jax.ShapeDtypeStruct((4, KS), F32), jax.ShapeDtypeStruct((4, LANES), F32)],
        interpret=interpret,
        name="finish",
    )(total)


def solution(mesh):
    fine = Mesh(mesh.devices.reshape(4, 8, 4, 2, 2), ALL)
    signal = P(CTX, MP)
    taps = P(None, CTX)
    return jax.shard_map(
        shards,
        mesh=fine,
        in_specs=(signal,) * 4 + (taps,) * 2,
        out_specs=(signal,) * 3 + (taps,) * 2,
        check_vma=False,
    )
```

```python
import functools

import jax
import jax.numpy as jnp
from jax import lax
from jax.experimental import pallas as pl
from jax.experimental.pallas import tpu as pltpu
from jax.sharding import Mesh, PartitionSpec as P

F32 = jnp.float32
BF16 = jnp.bfloat16
CPG = 16
KS = 7
KB = 128
LANES = 128
GPB = LANES // CPG
HALO = 8
CTX = ("x", "z", "yh")
MP = ("yl", "core")
ALL = CTX + MP
SIZES = (4, 8, 4, 4)
VMEM = 12 * 1024 * 1024


def params(**more):
    return pltpu.CompilerParams(vmem_limit_bytes=VMEM, **more)


def lane_group(shape):
    return lax.broadcasted_iota(jnp.int32, shape, len(shape) - 1) // CPG


def short_taps(taps):
    row = lax.broadcasted_iota(jnp.int32, (16, LANES), 0)
    group = jnp.where(row % 8 >= 4, row // 8 * 4 + row % 4, -1)
    spread = (lane_group((16, LANES)) == group).astype(BF16)
    return lax.dot_general(taps, spread, (((0,), (0,)), ((), ())), preferred_element_type=F32)[:8]


def fused_kernel(q, k, v, g, below, above, taps, *refs):
    gq, gk, gv, part, qs, ks, vs, feats = refs[-8:]
    rows = gq.shape[0]
    near = rows + 8
    both = taps[...].reshape(16, LANES)
    h = short_taps(both)
    early, late = below[...].astype(F32), above[...].astype(F32)
    made = []
    for i, (slot, x) in enumerate(((ks, k), (vs, v), (qs, q))):
        slot[0:8] = early[KB + 8 * i : KB + 8 * i + 8]
        slot[8:near] = x[...].astype(F32)[:rows]
        slot[near : near + 8] = late[KB + 8 * i : KB + 8 * i + 8]
        made.append(causal(h, slot, near))
    kf, vf, qf = made
    gate = jnp.concatenate([g[...].astype(F32)[:rows], late[KB + 24 :]], 0)
    uw = jnp.concatenate([early[:KB], kf * vf], 0)
    dw = jnp.concatenate([gate * qf, late[:KB]], 0)
    u_low, u_high = uw[: 2 * KB].astype(BF16), uw[16:].astype(BF16)
    d_low, d_high = dw[: 2 * KB].astype(BF16), dw[16:].astype(BF16)
    own = jnp.concatenate([dw[:rows], jnp.zeros((8, LANES), F32)], 0).astype(BF16)

    at = lax.broadcasted_iota(jnp.int32, (LANES, LANES), 0)
    to = lax.broadcasted_iota(jnp.int32, (LANES, LANES), 1)
    flip = (at + to == LANES - 1).astype(BF16)
    straight = both.astype(F32)
    turned = jnp.dot(both, flip, preferred_element_type=F32)
    lane = lax.broadcasted_iota(jnp.int32, (16, LANES), 1)
    row = lax.broadcasted_iota(jnp.int32, (16, LANES), 0)
    lane8, row8 = lane[:8], row[:8]
    contract = (((1,), (1,)), ((), ()))
    wide = lane_group((2 * KB, LANES))

    def square(line, first):
        base = pltpu.roll(jnp.broadcast_to(line, (16, LANES)), first, 1, stride=1, stride_axis=0)
        tiles = []
        for a in range(KB // 16):
            tile = pltpu.roll(base, 16 * a, 1) if a else base
            upper = lane > row + 16 * a if first else lane >= row + 16 * a
            parts = [jnp.where(upper, tile, 0.0), jnp.where(upper, 0.0, tile)]
            tiles.append(jnp.concatenate(parts, 1).astype(BF16))
        return tiles

    z_low = du_high = jnp.zeros((KB, LANES), F32)
    tails, heads, medium = [], [], []
    rest = jnp.concatenate([jnp.where(wide[:16] == i, own[KB:], 0) for i in range(GPB)], 0)
    last = lax.dot_general(rest, u_high, contract, preferred_element_type=F32)
    for i in range(GPB):
        line = i // 4 * 8 + i % 4
        tc = square(turned[line : line + 1], 1)
        ta = square(straight[line : line + 1], 0)
        tails.append(tc[-1])
        heads.append(ta[0])
        z_low = z_low + jnp.dot(
            jnp.concatenate(tc, 0), jnp.where(wide == i, u_low, 0), preferred_element_type=F32
        )
        du_high = du_high + jnp.dot(
            jnp.concatenate(ta, 0), jnp.where(wide == i, d_high, 0), preferred_element_type=F32
        )
        mine = jnp.where(wide[:KB] == i, own[:KB], 0)
        prod = lax.dot_general(mine, u_low, contract, preferred_element_type=F32)
        total = None
        for a in range(KB // 8):
            tile = prod[8 * a : 8 * a + 8]
            if a == KB // 8 - 2:
                tile = tile + last[16 * i : 16 * i + 8]
            tile = jnp.where(lane8 > row8 + 8 * a, tile[:, :KB], tile[:, KB:])
            total = tile if a == 0 else total + pltpu.roll(tile, KB - 8 * a, 1)
        medium.append(jnp.sum(align_left(total), 0, keepdims=True))
    for half in range(2):
        part[half, 0:4] = jnp.concatenate(medium[4 * half : 4 * half + 4], 0)

    z_high = pick_groups(
        jnp.dot(jnp.concatenate(tails, 0), u_high, preferred_element_type=F32), 16, 0, 16
    )
    du_low = pick_groups(
        jnp.dot(jnp.concatenate(heads, 0), d_low, preferred_element_type=F32), 16, 0, 16
    )
    z = jnp.concatenate([z_low, z_high], 0)
    du = jnp.concatenate([du_low, du_high], 0)
    feats[0] = (gate[:near] * z).astype(BF16).astype(F32)
    feats[1] = (du * vf).astype(BF16).astype(F32)
    feats[2] = (du * kf).astype(BF16).astype(F32)

    sums = [jnp.zeros((8, LANES), F32)] * 8
    for i, (slot, base, out) in enumerate(((qs, 8, gq), (ks, 8, gk), (vs, 8, gv))):
        wide_feat = feats[i, 0:rows]
        for j in range(KS):
            both_rows = wide_feat * slot[base - j : base - j + rows]
            sums[j] = sums[j] + jnp.sum(both_rows.reshape(rows // 8, 8, LANES), 0)
        total = h[0:1] * wide_feat
        for j in range(1, KS):
            total = total + h[j : j + 1] * feats[i, j : j + rows]
        out[...] = total.astype(BF16)
    short = jnp.concatenate([jnp.sum(x, 0, keepdims=True) for x in sums], 0)
    swapped = pltpu.roll(short, LANES // 2, 1)
    left = lane[:4] < LANES // 2
    part[0, 4:8] = jnp.where(left, short[:4], swapped[4:])
    part[1, 4:8] = jnp.where(left, swapped[:4], short[4:])


def fused(signals, rows, below, above, taps, first, count, written=(), interpret=False):
    channels = signals.shape[1]
    block = lambda r, n=0: pl.BlockSpec((r, LANES), lambda i: (n, first + i))
    sent = lambda r: pl.BlockSpec((r, LANES), lambda i: (0, i))
    chunk = pl.BlockSpec((2, 1, 8, LANES), lambda i: ((first + i) % 2, (first + i) // 2, 0, 0))
    return pl.pallas_call(
        fused_kernel,
        grid=(count,),
        in_specs=[block(signals.shape[0] // 4, n) for n in range(4)] + [sent(KB + 24), sent(KB + 32), chunk]
        + [pl.BlockSpec(memory_space=pl.ANY)] * len(written),
        out_specs=[block(rows)] * 3 + [pl.BlockSpec((2, 8, LANES), lambda i: (first + i, 0, 0))],
        out_shape=[jax.ShapeDtypeStruct((rows, channels), BF16)] * 3
        + [jax.ShapeDtypeStruct((channels // LANES * 2, 8, LANES), F32)],
        scratch_shapes=[pltpu.VMEM((rows + 16, LANES), F32)] * 3
        + [pltpu.VMEM((3, rows + 8, LANES), F32)],
        input_output_aliases={7 + n: n for n in range(len(written))},
        compiler_params=params(),
        cost_estimate=pl.CostEstimate(
            flops=250_000_000 * count, bytes_accessed=500_000 * count, transcendentals=0
        ),
        interpret=interpret,
        name="fused",
    )(*[signals] * 4, below, above, taps, *written)


def causal(h, slot, count):
    total = h[0:1] * slot[8 : 8 + count]
    for j in range(1, KS):
        total = total + h[j : j + 1] * slot[8 - j : 8 - j + count]
    return total.astype(BF16).astype(F32)


def products_kernel(q, k, v, g, taps, lower, upper, qs, ks, vs):
    rows = ks.shape[0]
    h = short_taps(taps[...].reshape(16, LANES))
    for slot, x in ((ks, k), (vs, v), (qs, q)):
        slot[...] = x[...].astype(F32)[:rows]
    kf, vf, qf = (causal(h, slot, KB) for slot in (ks, vs, qs))
    gate = g[...].astype(F32)[:rows]
    end = slice(rows - 8, rows)
    lower[...] = jnp.concatenate([kf * vf, ks[end], vs[end], qs[end]], 0).astype(BF16)
    upper[...] = jnp.concatenate([gate[8:] * qf, ks[0:8], vs[0:8], qs[0:8], gate[:8]], 0).astype(BF16)


def products(signals, rows, taps, first, count, interpret=False):
    assert rows == KB + 8
    block = lambda n: pl.BlockSpec((signals.shape[0] // 4, LANES), lambda i: (n, first + i))
    chunk = pl.BlockSpec((2, 1, 8, LANES), lambda i: ((first + i) % 2, (first + i) // 2, 0, 0))
    out = lambda r: pl.BlockSpec((r, LANES), lambda i: (0, i))
    return pl.pallas_call(
        products_kernel,
        grid=(count,),
        in_specs=[block(n) for n in range(4)] + [chunk],
        out_specs=[out(KB + 24), out(KB + 32)],
        out_shape=[jax.ShapeDtypeStruct((KB + r, count * LANES), BF16) for r in (24, 32)],
        scratch_shapes=[pltpu.VMEM((rows, LANES), F32)] * 3,
        compiler_params=params(),
        cost_estimate=pl.CostEstimate(flops=20_000_000, bytes_accessed=3_000_000, transcendentals=0),
        interpret=interpret,
        name="products",
    )(*[signals] * 4, taps)


def pick_groups(stacked, rows, start, count):
    groups = lane_group((count, LANES))
    out = stacked[start : start + count]
    for g in range(1, GPB):
        out = jnp.where(groups == g, stacked[g * rows + start : g * rows + start + count], out)
    return out


def align_left(tile):
    width = tile.shape[1]
    row = lax.broadcasted_iota(jnp.int32, tile.shape, 0)
    for bit in (1, 2, 4):
        tile = jnp.where(row // bit % 2 == 1, pltpu.roll(tile, width - bit, 1), tile)
    return tile


def step_ctx(value, step):
    count = lax.axis_size(CTX)
    return lax.ppermute(value, CTX, [(i, i + step) for i in range(count) if 0 <= i + step < count])


def turn(value, back=False):
    nx, nz, ny, nm = SIZES
    at = lambda x, z, y, m: ((x * nz + z) * ny + y) * nm + m
    pairs = [
        (at(x, z, y, m), at(y, z, m, x))
        for x in range(nx) for z in range(nz) for y in range(ny) for m in range(nm)
    ]
    if back:
        pairs = [(b, a) for a, b in pairs]
    return lax.ppermute(value, ALL, pairs)


def pack_taps(filt_short, filt_medium):
    short = jnp.pad(filt_short.T, ((0, 0), (0, LANES - KS)))
    return jnp.concatenate([filt_medium.T, short], 0)


def shards(q, k, v, g, filt_short, filt_medium):
    blocks = q.shape[1] // LANES
    rows = q.shape[0]
    pad = jnp.zeros((8, q.shape[1]), BF16)
    own, signals = lax.optimization_barrier((
        turn(pack_taps(filt_short, filt_medium)),
        jnp.concatenate([q, pad, k, pad, v, pad, g, pad], 0),
    ))
    taps = lax.all_to_all(
        jnp.broadcast_to(own[None], (32, 8, LANES)), ("x", "z"), 0, 0, tiled=True
    ).reshape(4, 8, 8, LANES)
    half = blocks // 2
    pieces = [(0, half), (half, blocks - half)]
    sent = []
    for first, count in pieces:
        lower, upper = products(signals, rows, taps, first, count)
        sent.append((step_ctx(lower, 1), step_ctx(upper, -1)))
    made = ()
    for (first, count), (below, above) in zip(pieces, sent):
        made = fused(signals, rows, below, above, taps, first, count, made)
    grad_q, grad_k, grad_v, part = made
    parts = lax.all_to_all(part, ("z", "yh"), 0, 0, tiled=True)
    goes = (jnp.arange(16) // 4 == lax.axis_index(MP)).astype(F32)
    spread = goes[:, None, None] * jnp.sum(parts, 0)
    arrived = lax.all_to_all(spread, ("x",) + MP, 0, 0, tiled=True)
    grad_short, grad_medium = finish(arrived)
    return grad_q, grad_k, grad_v, grad_short.T, grad_medium.T


def finish_kernel(arrived, short, medium):
    total = jnp.sum(arrived[...], 0)
    at = lax.broadcasted_iota(jnp.int32, (LANES, LANES), 0)
    to = lax.broadcasted_iota(jnp.int32, (LANES, LANES), 1)
    medium[...] = jnp.dot(
        total[0:4], ((at + to) % LANES == 0).astype(F32), precision=lax.Precision.HIGHEST,
        preferred_element_type=F32,
    )
    group = lax.broadcasted_iota(jnp.int32, (4, LANES), 0)
    halves = []
    for half in range(2):
        spread = (lane_group((4, LANES)) == group + 4 * half).astype(F32)
        halves.append(
            lax.dot_general(
                spread, total[4:8], (((1,), (1,)), ((), ())), precision=lax.Precision.HIGHEST,
                preferred_element_type=F32,
            )
        )
    short[...] = jnp.concatenate(halves, 1)[:, :KS]


def finish(total, interpret=False):
    return pl.pallas_call(
        finish_kernel,
        out_shape=[jax.ShapeDtypeStruct((4, KS), F32), jax.ShapeDtypeStruct((4, LANES), F32)],
        interpret=interpret,
        name="finish",
    )(total)


def solution(mesh):
    fine = Mesh(mesh.devices.reshape(4, 8, 4, 2, 2), ALL)
    signal = P(CTX, MP)
    taps = P(None, CTX)
    return jax.shard_map(
        shards,
        mesh=fine,
        in_specs=(signal,) * 4 + (taps,) * 2,
        out_specs=(signal,) * 3 + (taps,) * 2,
        check_vma=False,
    )
```

```python
import functools

import jax
import jax.numpy as jnp
from jax import lax
from jax.experimental import pallas as pl
from jax.experimental.pallas import tpu as pltpu
from jax.sharding import Mesh, PartitionSpec as P

F32 = jnp.float32
BF16 = jnp.bfloat16
CPG = 16
KS = 7
KB = 128
LANES = 128
GPB = LANES // CPG
HALO = 8
CTX = ("x", "z", "yh")
MP = ("yl", "core")
ALL = CTX + MP
SIZES = (4, 8, 4, 4)
WIDE = 2 * LANES
VMEM = 12 * 1024 * 1024


def params(**more):
    return pltpu.CompilerParams(vmem_limit_bytes=VMEM, **more)


def lane_group(shape):
    return lax.broadcasted_iota(jnp.int32, shape, len(shape) - 1) // CPG


def short_taps(taps):
    row = lax.broadcasted_iota(jnp.int32, (16, LANES), 0)
    group = jnp.where(row % 8 >= 4, row // 8 * 4 + row % 4, -1)
    spread = (lane_group((16, LANES)) == group).astype(BF16)
    return lax.dot_general(taps, spread, (((0,), (0,)), ((), ())), preferred_element_type=F32)[:8]


def fused_kernel(q, k, v, g, below, above, taps, *refs):
    gq, gk, gv, part, qs, ks, vs, feats = refs[-8:]
    for b in range(WIDE // LANES):
        lanes = slice(b * LANES, (b + 1) * LANES)
        one_block(
            *(x.at[:, lanes] for x in (q, k, v, g, below, above)), taps, b,
            *(x.at[:, lanes] for x in (gq, gk, gv)), part.at[2 * b : 2 * b + 2],
            qs.at[b], ks.at[b], vs.at[b], feats.at[b],
        )


def one_block(q, k, v, g, below, above, taps, b, gq, gk, gv, part, qs, ks, vs, feats):
    rows = gq.shape[0]
    near = rows + 8
    both = taps[2 * b : 2 * b + 2].reshape(16, LANES)
    h = short_taps(both)
    early, late = below[...].astype(F32), above[...].astype(F32)
    made = []
    for i, (slot, x) in enumerate(((ks, k), (vs, v), (qs, q))):
        slot[0:8] = early[KB + 8 * i : KB + 8 * i + 8]
        slot[8:near] = x[...].astype(F32)[:rows]
        slot[near : near + 8] = late[KB + 8 * i : KB + 8 * i + 8]
        made.append(causal(h, slot, near))
    kf, vf, qf = made
    gate = jnp.concatenate([g[...].astype(F32)[:rows], late[KB + 24 :]], 0)
    uw = jnp.concatenate([early[:KB], kf * vf], 0)
    dw = jnp.concatenate([gate * qf, late[:KB]], 0)

    part_rows = near // 2
    span = part_rows + KB
    blank = jnp.zeros((2 * KB - span, 2 * LANES), F32)

    def windows(x):
        pair = jnp.concatenate([x[:span], x[part_rows : part_rows + span]], 1)
        return jnp.concatenate([pair, blank], 0).astype(BF16)

    u_win, d_win = windows(uw), windows(dw)
    own = jnp.concatenate([dw[:rows], jnp.zeros((8, LANES), F32)], 0)
    own = jnp.concatenate([own[:part_rows], own[part_rows:]], 1)

    at = lax.broadcasted_iota(jnp.int32, (LANES, LANES), 0)
    to = lax.broadcasted_iota(jnp.int32, (LANES, LANES), 1)
    flip = (at + to == LANES - 1).astype(BF16)
    straight = both.astype(F32)
    turned = jnp.dot(both, flip, preferred_element_type=F32)
    lane = lax.broadcasted_iota(jnp.int32, (8, LANES), 1)
    row = lax.broadcasted_iota(jnp.int32, (8, LANES), 0)
    groups = jnp.concatenate([lane_group((part_rows, LANES))] * 2, 1)

    def squares(lines, first):
        tiles = []
        for i in range(GPB):
            line = lines[i // 4 * 8 + i % 4 : i // 4 * 8 + i % 4 + 1]
            base = pltpu.roll(jnp.broadcast_to(line, (8, LANES)), first, 1, stride=1, stride_axis=0)
            for a in range(part_rows // 8):
                tile = pltpu.roll(base, 8 * a, 1) if a else base
                upper = lane > row + 8 * a if first else lane >= row + 8 * a
                tiles.append(
                    jnp.concatenate([jnp.where(upper, tile, 0.0), jnp.where(upper, 0.0, tile)], 1)
                )
        return jnp.concatenate(tiles, 0).astype(BF16)

    def filtered(matrices, window):
        every = jnp.dot(matrices, window, preferred_element_type=F32)
        out = every[:part_rows]
        for i in range(1, GPB):
            out = jnp.where(groups == i, every[part_rows * i : part_rows * (i + 1)], out)
        return jnp.concatenate([out[:, :LANES], out[:, LANES:]], 0)

    z = filtered(squares(turned, 1), u_win)
    du = filtered(squares(straight, 0), d_win)

    mine = jnp.concatenate([jnp.where(groups == i, own, 0.0) for i in range(GPB)], 0).astype(BF16)
    prod = lax.dot_general(mine, u_win, (((1,), (1,)), ((), ())), preferred_element_type=F32)
    medium = []
    for i in range(GPB):
        total = None
        for a in range(part_rows // 8):
            tile = prod[part_rows * i + 8 * a : part_rows * i + 8 * a + 8]
            tile = jnp.where(lane > row + 8 * a, tile[:, :KB], tile[:, KB:])
            total = tile if a == 0 else total + pltpu.roll(tile, KB - 8 * a, 1)
        medium.append(jnp.sum(align_left(total), 0, keepdims=True))
    for half in range(2):
        part[half, 0:4] = jnp.concatenate(medium[4 * half : 4 * half + 4], 0)

    feats[0] = (gate[:near] * z).astype(BF16).astype(F32)
    feats[1] = (du * vf).astype(BF16).astype(F32)
    feats[2] = (du * kf).astype(BF16).astype(F32)

    sums = [jnp.zeros((8, LANES), F32)] * 8
    for i, (slot, base, out) in enumerate(((qs, 8, gq), (ks, 8, gk), (vs, 8, gv))):
        wide_feat = feats[i, 0:rows]
        for j in range(KS):
            both_rows = wide_feat * slot[base - j : base - j + rows]
            sums[j] = sums[j] + jnp.sum(both_rows.reshape(rows // 8, 8, LANES), 0)
        total = h[0:1] * wide_feat
        for j in range(1, KS):
            total = total + h[j : j + 1] * feats[i, j : j + rows]
        out[...] = total.astype(BF16)
    short = jnp.concatenate([jnp.sum(x, 0, keepdims=True) for x in sums], 0)
    swapped = pltpu.roll(short, LANES // 2, 1)
    left = lane[:4] < LANES // 2
    part[0, 4:8] = jnp.where(left, short[:4], swapped[4:])
    part[1, 4:8] = jnp.where(left, swapped[:4], short[4:])


def fused(signals, rows, below, above, taps, first, count, written=(), interpret=False):
    channels = signals.shape[1]
    block = lambda r, n=0: pl.BlockSpec((r, WIDE), lambda i: (n, first + i))
    sent = lambda r: pl.BlockSpec((r, WIDE), lambda i: (0, i))
    chunk = pl.BlockSpec((4, 1, 8, LANES), lambda i: (0, first + i, 0, 0))
    return pl.pallas_call(
        fused_kernel,
        grid=(count,),
        in_specs=[block(signals.shape[0] // 4, n) for n in range(4)] + [sent(KB + 24), sent(KB + 32), chunk]
        + [pl.BlockSpec(memory_space=pl.ANY)] * len(written),
        out_specs=[block(rows)] * 3 + [pl.BlockSpec((4, 8, LANES), lambda i: (first + i, 0, 0))],
        out_shape=[jax.ShapeDtypeStruct((rows, channels), BF16)] * 3
        + [jax.ShapeDtypeStruct((channels // LANES * 2, 8, LANES), F32)],
        scratch_shapes=[pltpu.VMEM((WIDE // LANES, rows + 16, LANES), F32)] * 3
        + [pltpu.VMEM((WIDE // LANES, 3, rows + 8, LANES), F32)],
        input_output_aliases={7 + n: n for n in range(len(written))},
        compiler_params=params(),
        cost_estimate=pl.CostEstimate(
            flops=500_000_000 * count, bytes_accessed=1_000_000 * count, transcendentals=0
        ),
        interpret=interpret,
        name="fused",
    )(*[signals] * 4, below, above, taps, *written)


def causal(h, slot, count):
    total = h[0:1] * slot[8 : 8 + count]
    for j in range(1, KS):
        total = total + h[j : j + 1] * slot[8 - j : 8 - j + count]
    return total.astype(BF16).astype(F32)


def products_kernel(q, k, v, g, taps, lower, upper, qs, ks, vs):
    for b in range(WIDE // LANES):
        lanes = slice(b * LANES, (b + 1) * LANES)
        one_product(
            *(x.at[:, lanes] for x in (q, k, v, g)), taps[2 * b : 2 * b + 2],
            lower.at[:, lanes], upper.at[:, lanes], qs.at[b], ks.at[b], vs.at[b],
        )


def one_product(q, k, v, g, taps, lower, upper, qs, ks, vs):
    rows = ks.shape[0]
    h = short_taps(taps.reshape(16, LANES))
    for slot, x in ((ks, k), (vs, v), (qs, q)):
        slot[...] = x[...].astype(F32)[:rows]
    kf, vf, qf = (causal(h, slot, KB) for slot in (ks, vs, qs))
    gate = g[...].astype(F32)[:rows]
    end = slice(rows - 8, rows)
    lower[...] = jnp.concatenate([kf * vf, ks[end], vs[end], qs[end]], 0).astype(BF16)
    upper[...] = jnp.concatenate([gate[8:] * qf, ks[0:8], vs[0:8], qs[0:8], gate[:8]], 0).astype(BF16)


def products(signals, rows, taps, first, count, interpret=False):
    assert rows == KB + 8
    block = lambda n: pl.BlockSpec((signals.shape[0] // 4, WIDE), lambda i: (n, first + i))
    chunk = pl.BlockSpec((4, 1, 8, LANES), lambda i: (0, first + i, 0, 0))
    out = lambda r: pl.BlockSpec((r, WIDE), lambda i: (0, i))
    return pl.pallas_call(
        products_kernel,
        grid=(count,),
        in_specs=[block(n) for n in range(4)] + [chunk],
        out_specs=[out(KB + 24), out(KB + 32)],
        out_shape=[jax.ShapeDtypeStruct((KB + r, count * WIDE), BF16) for r in (24, 32)],
        scratch_shapes=[pltpu.VMEM((WIDE // LANES, rows, LANES), F32)] * 3,
        compiler_params=params(),
        cost_estimate=pl.CostEstimate(flops=20_000_000, bytes_accessed=3_000_000, transcendentals=0),
        interpret=interpret,
        name="products",
    )(*[signals] * 4, taps)


def align_left(tile):
    width = tile.shape[1]
    row = lax.broadcasted_iota(jnp.int32, tile.shape, 0)
    for bit in (1, 2, 4):
        tile = jnp.where(row // bit % 2 == 1, pltpu.roll(tile, width - bit, 1), tile)
    return tile


def step_ctx(value, step):
    count = lax.axis_size(CTX)
    return lax.ppermute(value, CTX, [(i, i + step) for i in range(count) if 0 <= i + step < count])


def turn(value, back=False):
    nx, nz, ny, nm = SIZES
    at = lambda x, z, y, m: ((x * nz + z) * ny + y) * nm + m
    pairs = [
        (at(x, z, y, m), at(y, z, m, x))
        for x in range(nx) for z in range(nz) for y in range(ny) for m in range(nm)
    ]
    if back:
        pairs = [(b, a) for a, b in pairs]
    return lax.ppermute(value, ALL, pairs)


def pack_taps(filt_short, filt_medium):
    short = jnp.pad(filt_short.T, ((0, 0), (0, LANES - KS)))
    return jnp.concatenate([filt_medium.T, short], 0)


def shards(q, k, v, g, filt_short, filt_medium):
    blocks = q.shape[1] // WIDE
    rows = q.shape[0]
    pad = jnp.zeros((8, q.shape[1]), BF16)
    own, signals = lax.optimization_barrier((
        turn(pack_taps(filt_short, filt_medium)),
        jnp.concatenate([q, pad, k, pad, v, pad, g, pad], 0),
    ))
    taps = lax.all_to_all(
        jnp.broadcast_to(own[None], (32, 8, LANES)), ("x", "z"), 0, 0, tiled=True
    ).reshape(4, 8, 8, LANES)
    half = blocks // 2
    pieces = [(0, half), (half, blocks - half)]
    sent = []
    for first, count in pieces:
        lower, upper = products(signals, rows, taps, first, count)
        sent.append((step_ctx(lower, 1), step_ctx(upper, -1)))
    made = ()
    for (first, count), (below, above) in zip(pieces, sent):
        made = fused(signals, rows, below, above, taps, first, count, made)
    grad_q, grad_k, grad_v, part = made
    parts = lax.all_to_all(part, ("z", "yh"), 0, 0, tiled=True)
    goes = (jnp.arange(16) // 4 == lax.axis_index(MP)).astype(F32)
    spread = goes[:, None, None] * jnp.sum(parts, 0)
    arrived = lax.all_to_all(spread, ("x",) + MP, 0, 0, tiled=True)
    grad_short, grad_medium = finish(arrived)
    return grad_q, grad_k, grad_v, grad_short.T, grad_medium.T


def finish_kernel(arrived, short, medium):
    total = jnp.sum(arrived[...], 0)
    at = lax.broadcasted_iota(jnp.int32, (LANES, LANES), 0)
    to = lax.broadcasted_iota(jnp.int32, (LANES, LANES), 1)
    medium[...] = jnp.dot(
        total[0:4], ((at + to) % LANES == 0).astype(F32), precision=lax.Precision.HIGHEST,
        preferred_element_type=F32,
    )
    group = lax.broadcasted_iota(jnp.int32, (4, LANES), 0)
    halves = []
    for half in range(2):
        spread = (lane_group((4, LANES)) == group + 4 * half).astype(F32)
        halves.append(
            lax.dot_general(
                spread, total[4:8], (((1,), (1,)), ((), ())), precision=lax.Precision.HIGHEST,
                preferred_element_type=F32,
            )
        )
    short[...] = jnp.concatenate(halves, 1)[:, :KS]


def finish(total, interpret=False):
    return pl.pallas_call(
        finish_kernel,
        out_shape=[jax.ShapeDtypeStruct((4, KS), F32), jax.ShapeDtypeStruct((4, LANES), F32)],
        interpret=interpret,
        name="finish",
    )(total)


def solution(mesh):
    fine = Mesh(mesh.devices.reshape(4, 8, 4, 2, 2), ALL)
    signal = P(CTX, MP)
    taps = P(None, CTX)
    return jax.shard_map(
        shards,
        mesh=fine,
        in_specs=(signal,) * 4 + (taps,) * 2,
        out_specs=(signal,) * 3 + (taps,) * 2,
        check_vma=False,
    )
```

```python
import functools

import jax
import jax.numpy as jnp
from jax import lax
from jax.experimental import pallas as pl
from jax.experimental.pallas import tpu as pltpu
from jax.sharding import Mesh, PartitionSpec as P

F32 = jnp.float32
BF16 = jnp.bfloat16
CPG = 16
KS = 7
KB = 128
LANES = 128
GPB = LANES // CPG
STEP = 24
HALO = 8
CTX = ("x", "z", "yh")
MP = ("yl", "core")
ALL = CTX + MP
SIZES = (4, 8, 4, 4)
WIDE = 2 * LANES
VMEM = 12 * 1024 * 1024


def params(**more):
    return pltpu.CompilerParams(vmem_limit_bytes=VMEM, **more)


def lane_group(shape):
    return lax.broadcasted_iota(jnp.int32, shape, len(shape) - 1) // CPG


def short_taps(taps):
    row = lax.broadcasted_iota(jnp.int32, (16, LANES), 0)
    group = jnp.where(row % 8 >= 4, row // 8 * 4 + row % 4, -1)
    spread = (lane_group((16, LANES)) == group).astype(BF16)
    return lax.dot_general(taps, spread, (((0,), (0,)), ((), ())), preferred_element_type=F32)[:8]


def fused_kernel(q, k, v, g, below, above, taps, *refs):
    gq, gk, gv, part, qs, ks, vs, feats = refs[-8:]
    for b in range(WIDE // LANES):
        lanes = slice(b * LANES, (b + 1) * LANES)
        one_block(
            *(x.at[:, lanes] for x in (q, k, v, g, below, above)), taps, b,
            *(x.at[:, lanes] for x in (gq, gk, gv)), part.at[2 * b : 2 * b + 2],
            qs.at[b], ks.at[b], vs.at[b], feats.at[b],
        )


def one_block(q, k, v, g, below, above, taps, b, gq, gk, gv, part, qs, ks, vs, feats):
    rows = gq.shape[0]
    near = rows + 8
    both = taps[2 * b : 2 * b + 2].reshape(16, LANES)
    h = short_taps(both)
    early, late = below[...].astype(F32), above[...].astype(F32)
    made = []
    for i, (slot, x) in enumerate(((ks, k), (vs, v), (qs, q))):
        slot[0:8] = early[KB + 8 * i : KB + 8 * i + 8]
        slot[8:near] = x[...].astype(F32)[:rows]
        slot[near : near + 8] = late[KB + 8 * i : KB + 8 * i + 8]
        made.append(causal(h, slot, near))
    kf, vf, qf = made
    gate = jnp.concatenate([g[...].astype(F32)[:rows], late[KB + 24 :]], 0)
    uw = jnp.concatenate([early[:KB], kf * vf], 0)
    dw = jnp.concatenate([gate * qf, late[:KB]], 0)

    span = STEP + KB
    starts = range(0, near, STEP)
    blank = jnp.zeros((2 * KB - span, 2 * LANES), F32)

    def windows(x):
        pairs = [
            jnp.concatenate([x[t : t + span], x[t + STEP : t + STEP + span]], 1)
            for t in starts[::2]
        ]
        return [jnp.concatenate([pair, blank], 0).astype(BF16) for pair in pairs]

    u_win, d_win = windows(uw), windows(dw)
    own = jnp.concatenate([dw[:rows], jnp.zeros((8, LANES), F32)], 0)
    own = jnp.concatenate([own[t : t + STEP] for t in starts], 1)

    at = lax.broadcasted_iota(jnp.int32, (LANES, LANES), 0)
    to = lax.broadcasted_iota(jnp.int32, (LANES, LANES), 1)
    flip = (at + to == LANES - 1).astype(BF16)
    straight = both.astype(F32)
    turned = jnp.dot(both, flip, preferred_element_type=F32)
    lane = lax.broadcasted_iota(jnp.int32, (8, LANES), 1)
    row = lax.broadcasted_iota(jnp.int32, (8, LANES), 0)
    groups = jnp.concatenate([lane_group((STEP, LANES))] * len(starts), 1)

    def squares(lines, first):
        tiles = []
        for i in range(GPB):
            line = lines[i // 4 * 8 + i % 4 : i // 4 * 8 + i % 4 + 1]
            base = pltpu.roll(jnp.broadcast_to(line, (8, LANES)), first, 1, stride=1, stride_axis=0)
            for a in range(STEP // 8):
                tile = pltpu.roll(base, 8 * a, 1) if a else base
                upper = lane > row + 8 * a if first else lane >= row + 8 * a
                tiles.append(
                    jnp.concatenate([jnp.where(upper, tile, 0.0), jnp.where(upper, 0.0, tile)], 1)
                )
        return jnp.concatenate(tiles, 0).astype(BF16)

    def filtered(matrices, window):
        made = []
        for pair in window:
            every = jnp.dot(matrices, pair, preferred_element_type=F32)
            out = every[:STEP]
            for i in range(1, GPB):
                out = jnp.where(groups[:, : 2 * LANES] == i, every[STEP * i : STEP * (i + 1)], out)
            made += [out[:, :LANES], out[:, LANES:]]
        return jnp.concatenate(made, 0)

    z = filtered(squares(turned, 1), u_win)
    du = filtered(squares(straight, 0), d_win)

    mine = jnp.concatenate([jnp.where(groups == i, own, 0.0) for i in range(GPB)], 0).astype(BF16)
    prod = lax.dot_general(
        mine, jnp.concatenate(u_win, 1), (((1,), (1,)), ((), ())), preferred_element_type=F32
    )
    totals = []
    for i in range(GPB):
        for a in range(STEP // 8):
            tile = prod[STEP * i + 8 * a : STEP * i + 8 * a + 8]
            tile = jnp.where(lane > row + 8 * a, tile[:, :KB], tile[:, KB:])
            total = tile if a == 0 else total + pltpu.roll(tile, KB - 8 * a, 1)
        totals.append(total)
    aligned = align_left(jnp.concatenate(totals, 0))
    medium = jnp.sum(aligned.reshape(GPB, 8, LANES), 1)
    for half in range(2):
        part[half, 0:4] = medium[4 * half : 4 * half + 4]

    feats[0] = (gate[:near] * z).astype(BF16).astype(F32)
    feats[1] = (du * vf).astype(BF16).astype(F32)
    feats[2] = (du * kf).astype(BF16).astype(F32)

    sums = [jnp.zeros((8, LANES), F32)] * 8
    for i, (slot, base, out) in enumerate(((qs, 8, gq), (ks, 8, gk), (vs, 8, gv))):
        wide_feat = feats[i, 0:rows]
        for j in range(KS):
            both_rows = wide_feat * slot[base - j : base - j + rows]
            sums[j] = sums[j] + jnp.sum(both_rows.reshape(rows // 8, 8, LANES), 0)
        total = h[0:1] * wide_feat
        for j in range(1, KS):
            total = total + h[j : j + 1] * feats[i, j : j + rows]
        out[...] = total.astype(BF16)
    short = jnp.concatenate([jnp.sum(x, 0, keepdims=True) for x in sums], 0)
    swapped = pltpu.roll(short, LANES // 2, 1)
    left = lane[:4] < LANES // 2
    part[0, 4:8] = jnp.where(left, short[:4], swapped[4:])
    part[1, 4:8] = jnp.where(left, swapped[:4], short[4:])


def fused(signals, rows, below, above, taps, first, count, written=(), interpret=False):
    channels = signals.shape[1]
    block = lambda r, n=0: pl.BlockSpec((r, WIDE), lambda i: (n, first + i))
    sent = lambda r: pl.BlockSpec((r, WIDE), lambda i: (0, i))
    chunk = pl.BlockSpec((4, 1, 8, LANES), lambda i: (0, first + i, 0, 0))
    return pl.pallas_call(
        fused_kernel,
        grid=(count,),
        in_specs=[block(signals.shape[0] // 4, n) for n in range(4)] + [sent(KB + 24), sent(KB + 32), chunk]
        + [pl.BlockSpec(memory_space=pl.ANY)] * len(written),
        out_specs=[block(rows)] * 3 + [pl.BlockSpec((4, 8, LANES), lambda i: (first + i, 0, 0))],
        out_shape=[jax.ShapeDtypeStruct((rows, channels), BF16)] * 3
        + [jax.ShapeDtypeStruct((channels // LANES * 2, 8, LANES), F32)],
        scratch_shapes=[pltpu.VMEM((WIDE // LANES, rows + 16, LANES), F32)] * 3
        + [pltpu.VMEM((WIDE // LANES, 3, rows + 8, LANES), F32)],
        input_output_aliases={7 + n: n for n in range(len(written))},
        compiler_params=params(),
        cost_estimate=pl.CostEstimate(
            flops=500_000_000 * count, bytes_accessed=1_000_000 * count, transcendentals=0
        ),
        interpret=interpret,
        name="fused",
    )(*[signals] * 4, below, above, taps, *written)


def causal(h, slot, count):
    total = h[0:1] * slot[8 : 8 + count]
    for j in range(1, KS):
        total = total + h[j : j + 1] * slot[8 - j : 8 - j + count]
    return total.astype(BF16).astype(F32)


def products_kernel(q, k, v, g, taps, lower, upper, qs, ks, vs):
    for b in range(WIDE // LANES):
        lanes = slice(b * LANES, (b + 1) * LANES)
        one_product(
            *(x.at[:, lanes] for x in (q, k, v, g)), taps[2 * b : 2 * b + 2],
            lower.at[:, lanes], upper.at[:, lanes], qs.at[b], ks.at[b], vs.at[b],
        )


def one_product(q, k, v, g, taps, lower, upper, qs, ks, vs):
    rows = ks.shape[0]
    h = short_taps(taps.reshape(16, LANES))
    for slot, x in ((ks, k), (vs, v), (qs, q)):
        slot[...] = x[...].astype(F32)[:rows]
    kf, vf, qf = (causal(h, slot, KB) for slot in (ks, vs, qs))
    gate = g[...].astype(F32)[:rows]
    end = slice(rows - 8, rows)
    lower[...] = jnp.concatenate([kf * vf, ks[end], vs[end], qs[end]], 0).astype(BF16)
    upper[...] = jnp.concatenate([gate[8:] * qf, ks[0:8], vs[0:8], qs[0:8], gate[:8]], 0).astype(BF16)


def products(signals, rows, taps, first, count, interpret=False):
    assert rows == KB + 8
    block = lambda n: pl.BlockSpec((signals.shape[0] // 4, WIDE), lambda i: (n, first + i))
    chunk = pl.BlockSpec((4, 1, 8, LANES), lambda i: (0, first + i, 0, 0))
    out = lambda r: pl.BlockSpec((r, WIDE), lambda i: (0, i))
    return pl.pallas_call(
        products_kernel,
        grid=(count,),
        in_specs=[block(n) for n in range(4)] + [chunk],
        out_specs=[out(KB + 24), out(KB + 32)],
        out_shape=[jax.ShapeDtypeStruct((KB + r, count * WIDE), BF16) for r in (24, 32)],
        scratch_shapes=[pltpu.VMEM((WIDE // LANES, rows, LANES), F32)] * 3,
        compiler_params=params(),
        cost_estimate=pl.CostEstimate(flops=20_000_000, bytes_accessed=3_000_000, transcendentals=0),
        interpret=interpret,
        name="products",
    )(*[signals] * 4, taps)


def align_left(tile):
    width = tile.shape[1]
    row = lax.broadcasted_iota(jnp.int32, tile.shape, 0)
    for bit in (1, 2, 4):
        tile = jnp.where(row // bit % 2 == 1, pltpu.roll(tile, width - bit, 1), tile)
    return tile


def step_ctx(value, step):
    count = lax.axis_size(CTX)
    return lax.ppermute(value, CTX, [(i, i + step) for i in range(count) if 0 <= i + step < count])


def turn(value, back=False):
    nx, nz, ny, nm = SIZES
    at = lambda x, z, y, m: ((x * nz + z) * ny + y) * nm + m
    pairs = [
        (at(x, z, y, m), at(y, z, m, x))
        for x in range(nx) for z in range(nz) for y in range(ny) for m in range(nm)
    ]
    if back:
        pairs = [(b, a) for a, b in pairs]
    return lax.ppermute(value, ALL, pairs)


def pack_taps(filt_short, filt_medium):
    short = jnp.pad(filt_short.T, ((0, 0), (0, LANES - KS)))
    return jnp.concatenate([filt_medium.T, short], 0)


def shards(q, k, v, g, filt_short, filt_medium):
    blocks = q.shape[1] // WIDE
    rows = q.shape[0]
    pad = jnp.zeros((8, q.shape[1]), BF16)
    own, signals = lax.optimization_barrier((
        turn(pack_taps(filt_short, filt_medium)),
        jnp.concatenate([q, pad, k, pad, v, pad, g, pad], 0),
    ))
    taps = lax.all_to_all(
        jnp.broadcast_to(own[None], (32, 8, LANES)), ("x", "z"), 0, 0, tiled=True
    ).reshape(4, 8, 8, LANES)
    half = blocks // 2
    pieces = [(0, half), (half, blocks - half)]
    sent = []
    for first, count in pieces:
        lower, upper = products(signals, rows, taps, first, count)
        sent.append((step_ctx(lower, 1), step_ctx(upper, -1)))
    made = ()
    for (first, count), (below, above) in zip(pieces, sent):
        made = fused(signals, rows, below, above, taps, first, count, made)
    grad_q, grad_k, grad_v, part = made
    parts = lax.all_to_all(part, ("z", "yh"), 0, 0, tiled=True)
    goes = (jnp.arange(16) // 4 == lax.axis_index(MP)).astype(F32)
    spread = goes[:, None, None] * jnp.sum(parts, 0)
    arrived = lax.all_to_all(spread, ("x",) + MP, 0, 0, tiled=True)
    grad_short, grad_medium = finish(arrived)
    return grad_q, grad_k, grad_v, grad_short.T, grad_medium.T


def finish_kernel(arrived, short, medium):
    total = jnp.sum(arrived[...], 0)
    at = lax.broadcasted_iota(jnp.int32, (LANES, LANES), 0)
    to = lax.broadcasted_iota(jnp.int32, (LANES, LANES), 1)
    medium[...] = jnp.dot(
        total[0:4], ((at + to) % LANES == 0).astype(F32), precision=lax.Precision.HIGHEST,
        preferred_element_type=F32,
    )
    group = lax.broadcasted_iota(jnp.int32, (4, LANES), 0)
    halves = []
    for half in range(2):
        spread = (lane_group((4, LANES)) == group + 4 * half).astype(F32)
        halves.append(
            lax.dot_general(
                spread, total[4:8], (((1,), (1,)), ((), ())), precision=lax.Precision.HIGHEST,
                preferred_element_type=F32,
            )
        )
    short[...] = jnp.concatenate(halves, 1)[:, :KS]


def finish(total, interpret=False):
    return pl.pallas_call(
        finish_kernel,
        out_shape=[jax.ShapeDtypeStruct((4, KS), F32), jax.ShapeDtypeStruct((4, LANES), F32)],
        interpret=interpret,
        name="finish",
    )(total)


def solution(mesh):
    fine = Mesh(mesh.devices.reshape(4, 8, 4, 2, 2), ALL)
    signal = P(CTX, MP)
    taps = P(None, CTX)
    return jax.shard_map(
        shards,
        mesh=fine,
        in_specs=(signal,) * 4 + (taps,) * 2,
        out_specs=(signal,) * 3 + (taps,) * 2,
        check_vma=False,
    )
```

```python
import functools

import jax
import jax.numpy as jnp
from jax import lax
from jax.experimental import pallas as pl
from jax.experimental.pallas import tpu as pltpu
from jax.sharding import Mesh, PartitionSpec as P

F32 = jnp.float32
BF16 = jnp.bfloat16
CPG = 16
KS = 7
KB = 128
LANES = 128
GPB = LANES // CPG
STEP = 24
HALO = 8
CTX = ("x", "z", "yh")
MP = ("yl", "core")
ALL = CTX + MP
SIZES = (4, 8, 4, 4)
WIDE = 4 * LANES
VMEM = 12 * 1024 * 1024


def params(**more):
    return pltpu.CompilerParams(vmem_limit_bytes=VMEM, **more)


def lane_group(shape):
    return lax.broadcasted_iota(jnp.int32, shape, len(shape) - 1) // CPG


def short_taps(taps):
    row = lax.broadcasted_iota(jnp.int32, (16, LANES), 0)
    group = jnp.where(row % 8 >= 4, row // 8 * 4 + row % 4, -1)
    spread = (lane_group((16, LANES)) == group).astype(BF16)
    return lax.dot_general(taps, spread, (((0,), (0,)), ((), ())), preferred_element_type=F32)[:8]


def fused_kernel(q, k, v, g, below, above, taps, *refs):
    gq, gk, gv, part, qs, ks, vs, feats = refs[-8:]
    for b in range(WIDE // LANES):
        lanes = slice(b * LANES, (b + 1) * LANES)
        one_block(
            *(x.at[:, lanes] for x in (q, k, v, g, below, above)), taps, b,
            *(x.at[:, lanes] for x in (gq, gk, gv)), part.at[2 * b : 2 * b + 2],
            qs.at[b], ks.at[b], vs.at[b], feats.at[b],
        )


def one_block(q, k, v, g, below, above, taps, b, gq, gk, gv, part, qs, ks, vs, feats):
    rows = gq.shape[0]
    near = rows + 8
    both = taps[2 * (b % 2) : 2 * (b % 2) + 2, b // 2].reshape(16, LANES)
    h = short_taps(both)
    early, late = below[...].astype(F32), above[...].astype(F32)
    made = []
    for i, (slot, x) in enumerate(((ks, k), (vs, v), (qs, q))):
        slot[0:8] = early[KB + 8 * i : KB + 8 * i + 8]
        slot[8:near] = x[...].astype(F32)[:rows]
        slot[near : near + 8] = late[KB + 8 * i : KB + 8 * i + 8]
        made.append(causal(h, slot, near))
    kf, vf, qf = made
    gate = jnp.concatenate([g[...].astype(F32)[:rows], late[KB + 24 :]], 0)
    uw = jnp.concatenate([early[:KB], kf * vf], 0)
    dw = jnp.concatenate([gate * qf, late[:KB]], 0)

    span = STEP + KB
    starts = range(0, near, STEP)
    blank = jnp.zeros((2 * KB - span, 2 * LANES), F32)

    def windows(x):
        pairs = [
            jnp.concatenate([x[t : t + span], x[t + STEP : t + STEP + span]], 1)
            for t in starts[::2]
        ]
        return [jnp.concatenate([pair, blank], 0).astype(BF16) for pair in pairs]

    u_win, d_win = windows(uw), windows(dw)
    own = jnp.concatenate([dw[:rows], jnp.zeros((8, LANES), F32)], 0)
    own = jnp.concatenate([own[t : t + STEP] for t in starts], 1)

    at = lax.broadcasted_iota(jnp.int32, (LANES, LANES), 0)
    to = lax.broadcasted_iota(jnp.int32, (LANES, LANES), 1)
    flip = (at + to == LANES - 1).astype(BF16)
    straight = both.astype(F32)
    turned = jnp.dot(both, flip, preferred_element_type=F32)
    lane = lax.broadcasted_iota(jnp.int32, (8, LANES), 1)
    row = lax.broadcasted_iota(jnp.int32, (8, LANES), 0)
    groups = jnp.concatenate([lane_group((STEP, LANES))] * len(starts), 1)

    def squares(lines, first):
        tiles = []
        for i in range(GPB):
            line = lines[i // 4 * 8 + i % 4 : i // 4 * 8 + i % 4 + 1]
            base = pltpu.roll(jnp.broadcast_to(line, (8, LANES)), first, 1, stride=1, stride_axis=0)
            for a in range(STEP // 8):
                tile = pltpu.roll(base, 8 * a, 1) if a else base
                upper = lane > row + 8 * a if first else lane >= row + 8 * a
                tiles.append(
                    jnp.concatenate([jnp.where(upper, tile, 0.0), jnp.where(upper, 0.0, tile)], 1)
                )
        return jnp.concatenate(tiles, 0).astype(BF16)

    def filtered(matrices, window):
        made = []
        for pair in window:
            every = jnp.dot(matrices, pair, preferred_element_type=F32)
            out = every[:STEP]
            for i in range(1, GPB):
                out = jnp.where(groups[:, : 2 * LANES] == i, every[STEP * i : STEP * (i + 1)], out)
            made += [out[:, :LANES], out[:, LANES:]]
        return jnp.concatenate(made, 0)

    z = filtered(squares(turned, 1), u_win)
    du = filtered(squares(straight, 0), d_win)

    own = own.astype(BF16)
    mine = jnp.concatenate([jnp.where(groups == i, own, 0) for i in range(GPB)], 0)
    prod = lax.dot_general(
        mine, jnp.concatenate(u_win, 1), (((1,), (1,)), ((), ())), preferred_element_type=F32
    )
    totals = []
    for i in range(GPB):
        for a in range(STEP // 8):
            tile = prod[STEP * i + 8 * a : STEP * i + 8 * a + 8]
            tile = jnp.where(lane > row + 8 * a, tile[:, :KB], tile[:, KB:])
            total = tile if a == 0 else total + pltpu.roll(tile, KB - 8 * a, 1)
        totals.append(total)
    aligned = align_left(jnp.concatenate(totals, 0))
    medium = jnp.sum(aligned.reshape(GPB, 8, LANES), 1)
    for half in range(2):
        part[half, 0:4] = medium[4 * half : 4 * half + 4]

    feats[0] = (gate[:near] * z).astype(BF16).astype(F32)
    feats[1] = (du * vf).astype(BF16).astype(F32)
    feats[2] = (du * kf).astype(BF16).astype(F32)

    sums = [jnp.zeros((8, LANES), F32)] * 8
    for i, (slot, base, out) in enumerate(((qs, 8, gq), (ks, 8, gk), (vs, 8, gv))):
        wide_feat = feats[i, 0:rows]
        for j in range(KS):
            both_rows = wide_feat * slot[base - j : base - j + rows]
            sums[j] = sums[j] + jnp.sum(both_rows.reshape(rows // 8, 8, LANES), 0)
        total = h[0:1] * wide_feat
        for j in range(1, KS):
            total = total + h[j : j + 1] * feats[i, j : j + rows]
        out[...] = total.astype(BF16)
    short = jnp.concatenate([jnp.sum(x, 0, keepdims=True) for x in sums], 0)
    swapped = pltpu.roll(short, LANES // 2, 1)
    left = lane[:4] < LANES // 2
    part[0, 4:8] = jnp.where(left, short[:4], swapped[4:])
    part[1, 4:8] = jnp.where(left, swapped[:4], short[4:])


def fused(signals, rows, below, above, taps, first, count, written=(), interpret=False):
    channels = signals.shape[1]
    block = lambda r, n=0: pl.BlockSpec((r, WIDE), lambda i: (n, first + i))
    sent = lambda r: pl.BlockSpec((r, WIDE), lambda i: (0, i))
    chunk = pl.BlockSpec((4, WIDE // LANES // 2, 8, LANES), lambda i: (0, first + i, 0, 0))
    return pl.pallas_call(
        fused_kernel,
        grid=(count,),
        in_specs=[block(signals.shape[0] // 4, n) for n in range(4)] + [sent(KB + 24), sent(KB + 32), chunk]
        + [pl.BlockSpec(memory_space=pl.ANY)] * len(written),
        out_specs=[block(rows)] * 3 + [pl.BlockSpec((WIDE // LANES * 2, 8, LANES), lambda i: (first + i, 0, 0))],
        out_shape=[jax.ShapeDtypeStruct((rows, channels), BF16)] * 3
        + [jax.ShapeDtypeStruct((channels // LANES * 2, 8, LANES), F32)],
        scratch_shapes=[pltpu.VMEM((WIDE // LANES, rows + 16, LANES), F32)] * 3
        + [pltpu.VMEM((WIDE // LANES, 3, rows + 8, LANES), F32)],
        input_output_aliases={7 + n: n for n in range(len(written))},
        compiler_params=params(),
        cost_estimate=pl.CostEstimate(
            flops=500_000_000 * count, bytes_accessed=1_000_000 * count, transcendentals=0
        ),
        interpret=interpret,
        name="fused",
    )(*[signals] * 4, below, above, taps, *written)


def causal(h, slot, count):
    total = h[0:1] * slot[8 : 8 + count]
    for j in range(1, KS):
        total = total + h[j : j + 1] * slot[8 - j : 8 - j + count]
    return total.astype(BF16).astype(F32)


def products_kernel(q, k, v, g, taps, lower, upper, qs, ks, vs):
    for b in range(WIDE // LANES):
        lanes = slice(b * LANES, (b + 1) * LANES)
        one_product(
            *(x.at[:, lanes] for x in (q, k, v, g)), taps[2 * (b % 2) : 2 * (b % 2) + 2, b // 2],
            lower.at[:, lanes], upper.at[:, lanes], qs.at[b], ks.at[b], vs.at[b],
        )


def one_product(q, k, v, g, taps, lower, upper, qs, ks, vs):
    rows = ks.shape[0]
    h = short_taps(taps.reshape(16, LANES))
    for slot, x in ((ks, k), (vs, v), (qs, q)):
        slot[...] = x[...].astype(F32)[:rows]
    kf, vf, qf = (causal(h, slot, KB) for slot in (ks, vs, qs))
    gate = g[...].astype(F32)[:rows]
    end = slice(rows - 8, rows)
    lower[...] = jnp.concatenate([kf * vf, ks[end], vs[end], qs[end]], 0).astype(BF16)
    upper[...] = jnp.concatenate([gate[8:] * qf, ks[0:8], vs[0:8], qs[0:8], gate[:8]], 0).astype(BF16)


def products(signals, rows, taps, first, count, interpret=False):
    assert rows == KB + 8
    block = lambda n: pl.BlockSpec((signals.shape[0] // 4, WIDE), lambda i: (n, first + i))
    chunk = pl.BlockSpec((4, WIDE // LANES // 2, 8, LANES), lambda i: (0, first + i, 0, 0))
    out = lambda r: pl.BlockSpec((r, WIDE), lambda i: (0, i))
    return pl.pallas_call(
        products_kernel,
        grid=(count,),
        in_specs=[block(n) for n in range(4)] + [chunk],
        out_specs=[out(KB + 24), out(KB + 32)],
        out_shape=[jax.ShapeDtypeStruct((KB + r, count * WIDE), BF16) for r in (24, 32)],
        scratch_shapes=[pltpu.VMEM((WIDE // LANES, rows, LANES), F32)] * 3,
        compiler_params=params(),
        cost_estimate=pl.CostEstimate(flops=20_000_000, bytes_accessed=3_000_000, transcendentals=0),
        interpret=interpret,
        name="products",
    )(*[signals] * 4, taps)


def align_left(tile):
    width = tile.shape[1]
    row = lax.broadcasted_iota(jnp.int32, tile.shape, 0)
    for bit in (1, 2, 4):
        tile = jnp.where(row // bit % 2 == 1, pltpu.roll(tile, width - bit, 1), tile)
    return tile


def step_ctx(value, step):
    count = lax.axis_size(CTX)
    return lax.ppermute(value, CTX, [(i, i + step) for i in range(count) if 0 <= i + step < count])


def turn(value, back=False):
    nx, nz, ny, nm = SIZES
    at = lambda x, z, y, m: ((x * nz + z) * ny + y) * nm + m
    pairs = [
        (at(x, z, y, m), at(y, z, m, x))
        for x in range(nx) for z in range(nz) for y in range(ny) for m in range(nm)
    ]
    if back:
        pairs = [(b, a) for a, b in pairs]
    return lax.ppermute(value, ALL, pairs)


def pack_taps(filt_short, filt_medium):
    short = jnp.pad(filt_short.T, ((0, 0), (0, LANES - KS)))
    return jnp.concatenate([filt_medium.T, short], 0)


def shards(q, k, v, g, filt_short, filt_medium):
    blocks = q.shape[1] // WIDE
    rows = q.shape[0]
    pad = jnp.zeros((8, q.shape[1]), BF16)
    own, signals = lax.optimization_barrier((
        turn(pack_taps(filt_short, filt_medium)),
        jnp.concatenate([q, pad, k, pad, v, pad, g, pad], 0),
    ))
    taps = lax.all_to_all(
        jnp.broadcast_to(own[None], (32, 8, LANES)), ("x", "z"), 0, 0, tiled=True
    ).reshape(4, 8, 8, LANES)
    half = blocks // 2
    pieces = [(0, half), (half, blocks - half)]
    sent = []
    for first, count in pieces:
        lower, upper = products(signals, rows, taps, first, count)
        sent.append((step_ctx(lower, 1), step_ctx(upper, -1)))
    made = ()
    for (first, count), (below, above) in zip(pieces, sent):
        made = fused(signals, rows, below, above, taps, first, count, made)
    grad_q, grad_k, grad_v, part = made
    parts = lax.all_to_all(part, ("z", "yh"), 0, 0, tiled=True)
    goes = (jnp.arange(16) // 4 == lax.axis_index(MP)).astype(F32)
    spread = goes[:, None, None] * jnp.sum(parts, 0)
    arrived = lax.all_to_all(spread, ("x",) + MP, 0, 0, tiled=True)
    grad_short, grad_medium = finish(arrived)
    return grad_q, grad_k, grad_v, grad_short.T, grad_medium.T


def finish_kernel(arrived, short, medium):
    total = jnp.sum(arrived[...], 0)
    at = lax.broadcasted_iota(jnp.int32, (LANES, LANES), 0)
    to = lax.broadcasted_iota(jnp.int32, (LANES, LANES), 1)
    medium[...] = jnp.dot(
        total[0:4], ((at + to) % LANES == 0).astype(F32), precision=lax.Precision.HIGHEST,
        preferred_element_type=F32,
    )
    group = lax.broadcasted_iota(jnp.int32, (4, LANES), 0)
    halves = []
    for half in range(2):
        spread = (lane_group((4, LANES)) == group + 4 * half).astype(F32)
        halves.append(
            lax.dot_general(
                spread, total[4:8], (((1,), (1,)), ((), ())), precision=lax.Precision.HIGHEST,
                preferred_element_type=F32,
            )
        )
    short[...] = jnp.concatenate(halves, 1)[:, :KS]


def finish(total, interpret=False):
    return pl.pallas_call(
        finish_kernel,
        out_shape=[jax.ShapeDtypeStruct((4, KS), F32), jax.ShapeDtypeStruct((4, LANES), F32)],
        interpret=interpret,
        name="finish",
    )(total)


def solution(mesh):
    fine = Mesh(mesh.devices.reshape(4, 8, 4, 2, 2), ALL)
    signal = P(CTX, MP)
    taps = P(None, CTX)
    return jax.shard_map(
        shards,
        mesh=fine,
        in_specs=(signal,) * 4 + (taps,) * 2,
        out_specs=(signal,) * 3 + (taps,) * 2,
        check_vma=False,
    )
```

```python
import functools

import jax
import jax.numpy as jnp
from jax import lax
from jax.experimental import pallas as pl
from jax.experimental.pallas import tpu as pltpu
from jax.sharding import Mesh, PartitionSpec as P

F32 = jnp.float32
BF16 = jnp.bfloat16
CPG = 16
KS = 7
KB = 128
LANES = 128
GPB = LANES // CPG
STEP = 24
HALO = 8
CTX = ("x", "z", "yh")
MP = ("yl", "core")
ALL = CTX + MP
SIZES = (4, 8, 4, 4)
WIDE = 4 * LANES
VMEM = 12 * 1024 * 1024


def params(**more):
    return pltpu.CompilerParams(vmem_limit_bytes=VMEM, **more)


def lane_group(shape):
    return lax.broadcasted_iota(jnp.int32, shape, len(shape) - 1) // CPG


def short_taps(taps):
    row = lax.broadcasted_iota(jnp.int32, (16, LANES), 0)
    group = jnp.where(row % 8 >= 4, row // 8 * 4 + row % 4, -1)
    spread = (lane_group((16, LANES)) == group).astype(BF16)
    return lax.dot_general(taps, spread, (((0,), (0,)), ((), ())), preferred_element_type=F32)[:8]


def fused_kernel(q, k, v, g, below, above, taps, *refs):
    gq, gk, gv, part, qs, ks, vs, feats = refs[-8:]
    for b in range(WIDE // LANES):
        lanes = slice(b * LANES, (b + 1) * LANES)
        one_block(
            *(x.at[:, lanes] for x in (q, k, v, g, below, above)), taps, b,
            *(x.at[:, lanes] for x in (gq, gk, gv)), part.at[2 * b : 2 * b + 2],
            qs.at[b], ks.at[b], vs.at[b], feats.at[b],
        )


def one_block(q, k, v, g, below, above, taps, b, gq, gk, gv, part, qs, ks, vs, feats):
    rows = gq.shape[0]
    near = rows + 8
    both = taps[2 * (b % 2) : 2 * (b % 2) + 2, b // 2].reshape(16, LANES)
    h = short_taps(both)
    early, late = below[...].astype(F32), above[...].astype(F32)
    made = []
    for i, (slot, x) in enumerate(((ks, k), (vs, v), (qs, q))):
        slot[0:8] = early[KB + 8 * i : KB + 8 * i + 8]
        slot[8:near] = x[...].astype(F32)[:rows]
        slot[near : near + 8] = late[KB + 8 * i : KB + 8 * i + 8]
        made.append(causal(h, slot, near))
    kf, vf, qf = made
    gate = jnp.concatenate([g[...].astype(F32)[:rows], late[KB + 24 :]], 0)
    uw = jnp.concatenate([early[:KB], kf * vf], 0)
    dw = jnp.concatenate([gate * qf, late[:KB]], 0)

    span = STEP + KB
    starts = range(0, near, STEP)
    blank = jnp.zeros((2 * KB - span, 2 * LANES), F32)

    def windows(x):
        pairs = [
            jnp.concatenate([x[t : t + span], x[t + STEP : t + STEP + span]], 1)
            for t in starts[::2]
        ]
        return [jnp.concatenate([pair, blank], 0).astype(BF16) for pair in pairs]

    u_win, d_win = windows(uw), windows(dw)
    own = jnp.concatenate([dw[:rows], jnp.zeros((8, LANES), F32)], 0)
    own = jnp.concatenate([own[t : t + STEP] for t in starts], 1)

    at = lax.broadcasted_iota(jnp.int32, (LANES, LANES), 0)
    to = lax.broadcasted_iota(jnp.int32, (LANES, LANES), 1)
    flip = (at + to == LANES - 1).astype(BF16)
    straight = both.astype(F32)
    turned = jnp.dot(both, flip, preferred_element_type=F32)
    lane = lax.broadcasted_iota(jnp.int32, (8, LANES), 1)
    row = lax.broadcasted_iota(jnp.int32, (8, LANES), 0)
    groups = jnp.concatenate([lane_group((STEP, LANES))] * len(starts), 1)

    def squares(lines, first):
        tiles = []
        for i in range(GPB):
            line = lines[i // 4 * 8 + i % 4 : i // 4 * 8 + i % 4 + 1]
            base = pltpu.roll(jnp.broadcast_to(line, (8, LANES)), first, 1, stride=1, stride_axis=0)
            for a in range(STEP // 8):
                tile = pltpu.roll(base, 8 * a, 1) if a else base
                upper = lane > row + 8 * a if first else lane >= row + 8 * a
                tiles.append(
                    jnp.concatenate([jnp.where(upper, tile, 0.0), jnp.where(upper, 0.0, tile)], 1)
                )
        return jnp.concatenate(tiles, 0).astype(BF16)

    def filtered(matrices, window):
        made = []
        for pair in window:
            every = jnp.dot(matrices, pair, preferred_element_type=F32)
            out = every[:STEP]
            for i in range(1, GPB):
                out = jnp.where(groups[:, : 2 * LANES] == i, every[STEP * i : STEP * (i + 1)], out)
            made += [out[:, :LANES], out[:, LANES:]]
        return jnp.concatenate(made, 0)

    z = filtered(squares(turned, 1), u_win)
    du = filtered(squares(straight, 0), d_win)

    own = own.astype(BF16)
    mine = jnp.concatenate([jnp.where(groups == i, own, 0) for i in range(GPB)], 0)
    prod = lax.dot_general(
        mine, jnp.concatenate(u_win, 1), (((1,), (1,)), ((), ())), preferred_element_type=F32
    )
    totals = []
    for i in range(GPB):
        for a in range(STEP // 8):
            tile = prod[STEP * i + 8 * a : STEP * i + 8 * a + 8]
            tile = jnp.where(lane > row + 8 * a, tile[:, :KB], tile[:, KB:])
            total = tile if a == 0 else total + pltpu.roll(tile, KB - 8 * a, 1)
        totals.append(total)
    aligned = align_left(jnp.concatenate(totals, 0))
    medium = jnp.sum(aligned.reshape(GPB, 8, LANES), 1)
    for i in range(GPB):
        part[i // 4, :, LANES * (i % 4) : LANES * (i % 4 + 1)] = medium[i : i + 1]

    feats[0] = (gate[:near] * z).astype(BF16).astype(F32)
    feats[1] = (du * vf).astype(BF16).astype(F32)
    feats[2] = (du * kf).astype(BF16).astype(F32)

    sums = [jnp.zeros((8, LANES), F32)] * 8
    for i, (slot, base, out) in enumerate(((qs, 8, gq), (ks, 8, gk), (vs, 8, gv))):
        wide_feat = feats[i, 0:rows]
        for j in range(KS):
            both_rows = wide_feat * slot[base - j : base - j + rows]
            sums[j] = sums[j] + jnp.sum(both_rows.reshape(rows // 8, 8, LANES), 0)
        total = h[0:1] * wide_feat
        for j in range(1, KS):
            total = total + h[j : j + 1] * feats[i, j : j + rows]
        out[...] = total.astype(BF16)
    short = jnp.concatenate([jnp.sum(x, 0, keepdims=True) for x in sums], 0)
    for step in (8, 4, 2, 1):
        short = short + pltpu.roll(short, LANES - step, 1)
    short = pltpu.roll(short, 0, 1, stride=1, stride_axis=0)
    line = jnp.sum(jnp.where(lane % CPG == row, short, 0.0), 0, keepdims=True)
    part[0, :, 4 * LANES :] = line
    part[1, :, 4 * LANES :] = pltpu.roll(line, LANES // 2, 1)


def fused(signals, rows, below, above, taps, first, count, written=(), interpret=False):
    channels = signals.shape[1]
    block = lambda r, n=0: pl.BlockSpec((r, WIDE), lambda i: (n, first + i))
    sent = lambda r: pl.BlockSpec((r, WIDE), lambda i: (0, i))
    chunk = pl.BlockSpec((4, WIDE // LANES // 2, 8, LANES), lambda i: (0, first + i, 0, 0))
    return pl.pallas_call(
        fused_kernel,
        grid=(count,),
        in_specs=[block(signals.shape[0] // 4, n) for n in range(4)] + [sent(KB + 24), sent(KB + 32), chunk]
        + [pl.BlockSpec(memory_space=pl.ANY)] * len(written),
        out_specs=[block(rows)] * 3 + [pl.BlockSpec((WIDE // LANES * 2, 1, 5 * LANES), lambda i: (first + i, 0, 0))],
        out_shape=[jax.ShapeDtypeStruct((rows, channels), BF16)] * 3
        + [jax.ShapeDtypeStruct((channels // LANES * 2, 1, 5 * LANES), F32)],
        scratch_shapes=[pltpu.VMEM((WIDE // LANES, rows + 16, LANES), F32)] * 3
        + [pltpu.VMEM((WIDE // LANES, 3, rows + 8, LANES), F32)],
        input_output_aliases={7 + n: n for n in range(len(written))},
        compiler_params=params(),
        cost_estimate=pl.CostEstimate(
            flops=500_000_000 * count, bytes_accessed=1_000_000 * count, transcendentals=0
        ),
        interpret=interpret,
        name="fused",
    )(*[signals] * 4, below, above, taps, *written)


def causal(h, slot, count):
    total = h[0:1] * slot[8 : 8 + count]
    for j in range(1, KS):
        total = total + h[j : j + 1] * slot[8 - j : 8 - j + count]
    return total.astype(BF16).astype(F32)


def products_kernel(q, k, v, g, taps, lower, upper, qs, ks, vs):
    for b in range(WIDE // LANES):
        lanes = slice(b * LANES, (b + 1) * LANES)
        one_product(
            *(x.at[:, lanes] for x in (q, k, v, g)), taps[2 * (b % 2) : 2 * (b % 2) + 2, b // 2],
            lower.at[:, lanes], upper.at[:, lanes], qs.at[b], ks.at[b], vs.at[b],
        )


def one_product(q, k, v, g, taps, lower, upper, qs, ks, vs):
    rows = ks.shape[0]
    h = short_taps(taps.reshape(16, LANES))
    for slot, x in ((ks, k), (vs, v), (qs, q)):
        slot[...] = x[...].astype(F32)[:rows]
    kf, vf, qf = (causal(h, slot, KB) for slot in (ks, vs, qs))
    gate = g[...].astype(F32)[:rows]
    end = slice(rows - 8, rows)
    lower[...] = jnp.concatenate([kf * vf, ks[end], vs[end], qs[end]], 0).astype(BF16)
    upper[...] = jnp.concatenate([gate[8:] * qf, ks[0:8], vs[0:8], qs[0:8], gate[:8]], 0).astype(BF16)


def products(signals, rows, taps, first, count, interpret=False):
    assert rows == KB + 8
    block = lambda n: pl.BlockSpec((signals.shape[0] // 4, WIDE), lambda i: (n, first + i))
    chunk = pl.BlockSpec((4, WIDE // LANES // 2, 8, LANES), lambda i: (0, first + i, 0, 0))
    out = lambda r: pl.BlockSpec((r, WIDE), lambda i: (0, i))
    return pl.pallas_call(
        products_kernel,
        grid=(count,),
        in_specs=[block(n) for n in range(4)] + [chunk],
        out_specs=[out(KB + 24), out(KB + 32)],
        out_shape=[jax.ShapeDtypeStruct((KB + r, count * WIDE), BF16) for r in (24, 32)],
        scratch_shapes=[pltpu.VMEM((WIDE // LANES, rows, LANES), F32)] * 3,
        compiler_params=params(),
        cost_estimate=pl.CostEstimate(flops=20_000_000, bytes_accessed=3_000_000, transcendentals=0),
        interpret=interpret,
        name="products",
    )(*[signals] * 4, taps)


def align_left(tile):
    width = tile.shape[1]
    row = lax.broadcasted_iota(jnp.int32, tile.shape, 0)
    for bit in (1, 2, 4):
        tile = jnp.where(row // bit % 2 == 1, pltpu.roll(tile, width - bit, 1), tile)
    return tile


def step_ctx(value, step):
    count = lax.axis_size(CTX)
    return lax.ppermute(value, CTX, [(i, i + step) for i in range(count) if 0 <= i + step < count])


def turn(value, back=False):
    nx, nz, ny, nm = SIZES
    at = lambda x, z, y, m: ((x * nz + z) * ny + y) * nm + m
    pairs = [
        (at(x, z, y, m), at(y, z, m, x))
        for x in range(nx) for z in range(nz) for y in range(ny) for m in range(nm)
    ]
    if back:
        pairs = [(b, a) for a, b in pairs]
    return lax.ppermute(value, ALL, pairs)


def pack_taps(filt_short, filt_medium):
    short = jnp.pad(filt_short.T, ((0, 0), (0, LANES - KS)))
    return jnp.concatenate([filt_medium.T, short], 0)


def shards(q, k, v, g, filt_short, filt_medium):
    blocks = q.shape[1] // WIDE
    rows = q.shape[0]
    pad = jnp.zeros((8, q.shape[1]), BF16)
    own, signals = lax.optimization_barrier((
        turn(pack_taps(filt_short, filt_medium)),
        jnp.concatenate([q, pad, k, pad, v, pad, g, pad], 0),
    ))
    taps = lax.all_to_all(
        jnp.broadcast_to(own[None], (32, 8, LANES)), ("x", "z"), 0, 0, tiled=True
    ).reshape(4, 8, 8, LANES)
    half = blocks // 2
    pieces = [(0, half), (half, blocks - half)]
    sent = []
    for first, count in pieces:
        lower, upper = products(signals, rows, taps, first, count)
        sent.append((step_ctx(lower, 1), step_ctx(upper, -1)))
    made = ()
    for (first, count), (below, above) in zip(pieces, sent):
        made = fused(signals, rows, below, above, taps, first, count, made)
    grad_q, grad_k, grad_v, part = made
    parts = lax.all_to_all(part, ("z", "yh"), 0, 0, tiled=True)
    goes = (jnp.arange(16) // 4 == lax.axis_index(MP)).astype(F32)
    spread = goes[:, None, None] * jnp.sum(parts, 0)
    arrived = lax.all_to_all(spread, ("x",) + MP, 0, 0, tiled=True)
    grad_short, grad_medium = finish(arrived)
    return grad_q, grad_k, grad_v, grad_short.T, grad_medium.T


def finish_kernel(arrived, short, medium):
    total = jnp.sum(arrived[...], 0)
    rows = jnp.concatenate([total[:, LANES * i : LANES * (i + 1)] for i in range(4)], 0)
    at = lax.broadcasted_iota(jnp.int32, (LANES, LANES), 0)
    to = lax.broadcasted_iota(jnp.int32, (LANES, LANES), 1)
    medium[...] = jnp.dot(
        rows, ((at + to) % LANES == 0).astype(F32), precision=lax.Precision.HIGHEST,
        preferred_element_type=F32,
    )
    group = lax.broadcasted_iota(jnp.int32, (4, LANES), 0)
    line = jnp.broadcast_to(total[:, 4 * LANES :], (4, LANES))
    short[...] = jnp.dot(
        jnp.where(lane_group((4, LANES)) == group, line, 0.0), (at % CPG == to).astype(F32),
        precision=lax.Precision.HIGHEST, preferred_element_type=F32,
    )[:, :KS]


def finish(total, interpret=False):
    return pl.pallas_call(
        finish_kernel,
        out_shape=[jax.ShapeDtypeStruct((4, KS), F32), jax.ShapeDtypeStruct((4, LANES), F32)],
        interpret=interpret,
        name="finish",
    )(total)


def solution(mesh):
    fine = Mesh(mesh.devices.reshape(4, 8, 4, 2, 2), ALL)
    signal = P(CTX, MP)
    taps = P(None, CTX)
    return jax.shard_map(
        shards,
        mesh=fine,
        in_specs=(signal,) * 4 + (taps,) * 2,
        out_specs=(signal,) * 3 + (taps,) * 2,
        check_vma=False,
    )
```
